512 devices in a mesh: rep: 32 (over z_hi, y, core), shard: 16 (over z_lo, x).
Axes of the slice: x: 4, y: 8, z: 8 (z_hi: 2, z_lo: 4; z = z_hi * 4 + z_lo), core: 2. Of those that a mesh axis runs over, the one named last changes fastest.
Arguments:
- queries: bfloat16 [65536, 4096], P(('rep', 'shard')), may hold values from -120 to 120
- keys: bfloat16 [65536, 512], P(('rep', 'shard')), may hold values from -5.5 to 5.5
- grad_out: bfloat16 [65536, 4096], P(('rep', 'shard')), may hold values from -0.75 to 0.75
- inputs: bfloat16 [65536, 8192], P(('rep', 'shard')), may hold values from -6 to 6
- old_owner: int32 [64], replicated, may hold values from 0 to 11, as said below
- new_owner: int32 [64], replicated, may hold values from 0 to 15, as said below
- param_old: float32 [128, 96, 512], P('rep', 'shard'), may hold values from -0.75 to 0.75
- first_old: float32 [128, 96, 512], P('rep', 'shard'), may hold values from -6 to 6
- second_old: float32 [128, 96, 512], P('rep', 'shard'), may hold values from 0.5 to 20
Outputs:
- param_new: float32 [128, 64, 512], P('rep', 'shard')
- first_new: float32 [128, 64, 512], P('rep', 'shard')
- second_new: float32 [128, 64, 512], P('rep', 'shard')
- weights: bfloat16 [128, 64, 512], P('rep')
The draws below stay inside these ranges and needn't reach their ends.
Inputs may be any that keep to these rules, and one draw needn't show every extreme that they name: `old_owner`: each old owner holds at most 6 blocks, and some hold exactly 6. `new_owner`: each new owner holds exactly 4 blocks.
All inputs are finite; a program needn't handle non-finite values.
Results may differ from the reference program's by a relative error of at most 0.0034.
Values may be sent and summed in bfloat16 or wider, within the bound.
No kernel may reach another device: no remote copies, remote signals or barrier semaphores. Data moves between devices by JAX's collectives and lax.ppermute only.
A program may use at most 128 MiB of HBM per device.

```python
import math
import jax
import jax.numpy as jnp
from jax import lax

D = 8192
HEADS = 32
KV = 4
HD = 128
GRP = 8
LENGTH = 2048
TOKENS = 65536
BLOCKS = 64
BROWS = 128
OLD = 12
OLD_CAP = 6
NEW_CAP = 4
STEP = 1000
N_SHARD = 16


def paired_draw(key):
    seq_count = TOKENS // LENGTH
    key_values = jnp.clip(jax.random.normal(jax.random.fold_in(key, 11), (seq_count, LENGTH, KV, HD), jnp.float32), -4.5, 4.5)
    query_values = jnp.clip(jax.random.normal(jax.random.fold_in(key, 12), (seq_count, LENGTH, KV, GRP, HD), jnp.float32), -4.5, 4.5)
    return (query_values.reshape(TOKENS, HEADS * HD), key_values.reshape(TOKENS, KV * HD))


def draw_queries(key, part):
    return paired_draw(key)[0].astype(jnp.bfloat16)


def draw_keys(key, part):
    return paired_draw(key)[1].astype(jnp.bfloat16)


def draw_old_owner(key, part):
    shuffled = jax.random.permutation(jax.random.fold_in(key, 21), BLOCKS)
    inverse = jnp.argsort(shuffled)
    return (inverse % OLD).astype(jnp.int32)


def draw_new_owner(key, part):
    shuffled = jax.random.permutation(jax.random.fold_in(key, 22), BLOCKS)
    inverse = jnp.argsort(shuffled)
    return (inverse // NEW_CAP).astype(jnp.int32)


def shard_levels(own_key, shape, split, low, high):
    def one(axis_at, shards_of):
        heights = jax.random.uniform(jax.random.fold_in(jax.random.fold_in(own_key, 6), axis_at), (shards_of,), jnp.float32, low / len(split), high / len(split))
        return jnp.repeat(jnp.exp(heights), shape[axis_at] // shards_of).reshape((-1,) + (1,) * (len(shape) - axis_at - 1))

    level = one(*split[0])
    for cut in split[1:]:
        level = level * one(*cut)
    return level


def centred(own_key, dims, scale, most, shards=(), kind=jnp.bfloat16):
    entries = jax.random.normal(own_key, dims, jnp.float32) * scale
    if len(shards) > 0:
        entries = shard_levels(own_key, dims, shards, -0.22, 0.18) * entries
    return jnp.clip(entries, min=-most, max=most).astype(kind)


def setup_inputs(seed: int = 0) -> dict:
    splits = jax.random.split(jax.random.key(seed), 10)
    return {
        "queries": draw_queries(jax.random.fold_in(splits[9], 71), 0),
        "keys": draw_keys(jax.random.fold_in(splits[9], 71), 0),
        "grad_out": centred(splits[2], (TOKENS, HEADS * HD), (max(TOKENS // 1024, 1)) ** -0.5, 0.75, ((0, 512),)),
        "inputs": centred(splits[3], (TOKENS, D), 1.0, 6.0, ((0, 512),)),
        "old_owner": draw_old_owner(jax.random.fold_in(splits[9], 71), 0),
        "new_owner": draw_new_owner(jax.random.fold_in(splits[9], 71), 0),
        "param_old": centred(splits[6], (BROWS, N_SHARD * OLD_CAP, KV * HD), 0.05, 0.75, ((0, 32), (1, 16)), jnp.float32),
        "first_old": centred(splits[7], (BROWS, N_SHARD * OLD_CAP, KV * HD), 1.0, 6.0, ((0, 32), (1, 16)), jnp.float32),
        "second_old": jnp.clip(jnp.exp(math.log(20.0) - 3.6888795 * jax.random.uniform(splits[8], (BROWS, N_SHARD * OLD_CAP, KV * HD), jnp.float32) ** shard_levels(splits[8], (BROWS, N_SHARD * OLD_CAP, KV * HD), ((0, 32), (1, 16)), -0.2, 0.2)), 0.5, 20.0),
    }


beta_first = 0.9
beta_second = 0.95
learning_rate = 0.02
decay_rate = 0.1
epsilon = 1e-08

def owner_ranks(owner, owners):
    onehot = (owner[:, None] == jnp.arange(owners, dtype=jnp.int32)[None, :]).astype(jnp.int32)
    running = jnp.cumsum(onehot, axis=0)
    return (lax.optimization_barrier(jnp.sum(running * onehot, axis=1)) - 1).astype(jnp.int32)

def adamw(param, first, second, gradient):
    first = beta_first * first + (1.0 - beta_first) * gradient
    second = beta_second * second + (1.0 - beta_second) * gradient * gradient
    first_hat = first / (1.0 - beta_first ** STEP)
    second_hat = second / (1.0 - beta_second ** STEP)
    param = param - learning_rate * (first_hat / (jnp.sqrt(second_hat) + epsilon) + decay_rate * param)
    return (param, first, second)

def group_values(triple):
    query_block, key_block, cotangent = triple
    length = key_block.shape[0]
    scores = jnp.einsum('htd,ud->htu', query_block.astype(jnp.float32), key_block.astype(jnp.float32)) * HD ** (-0.5)
    allowed = jnp.arange(length)[None, :] <= jnp.arange(length)[:, None]
    scores = jnp.where(allowed[None], scores, -jnp.inf)
    highest = lax.optimization_barrier(jnp.max(scores, axis=-1, keepdims=True))
    weights = jnp.exp(scores - highest)
    probs = (weights / lax.optimization_barrier(jnp.sum(weights, axis=-1, keepdims=True))).astype(jnp.bfloat16)
    summed = jnp.einsum('htu,htd->ud', probs.astype(jnp.float32), cotangent.astype(jnp.float32))
    return summed.astype(jnp.bfloat16)

def sequence_values(triple):
    return lax.map(group_values, triple)

def reference(queries, keys, grad_out, inputs, old_owner, new_owner, param_old, first_old, second_old):
    seq_count = TOKENS // LENGTH
    query_groups = queries.reshape(seq_count, LENGTH, KV, GRP, HD).transpose(0, 2, 3, 1, 4)
    cotangent_groups = grad_out.reshape(seq_count, LENGTH, KV, GRP, HD).transpose(0, 2, 3, 1, 4)
    key_groups = keys.reshape(seq_count, LENGTH, KV, HD).transpose(0, 2, 1, 3)
    values = lax.map(sequence_values, (query_groups, key_groups, cotangent_groups))
    values = values.transpose(0, 2, 1, 3).reshape(TOKENS, KV * HD)
    gradient = lax.dot_general(inputs, values, (((0,), (0,)), ((), ())), preferred_element_type=jnp.float32)
    gradient = gradient.reshape(BLOCKS, BROWS, KV * HD).transpose(1, 0, 2)
    old_slot = (old_owner * OLD_CAP + owner_ranks(old_owner, N_SHARD)).astype(jnp.int32)
    param = jnp.take(param_old, old_slot, axis=1)
    first = jnp.take(first_old, old_slot, axis=1)
    second = jnp.take(second_old, old_slot, axis=1)
    param, first, second = adamw(param, first, second, gradient)
    new_slot = (new_owner * NEW_CAP + owner_ranks(new_owner, N_SHARD)).astype(jnp.int32)
    placing = jnp.argsort(new_slot).astype(jnp.int32)
    param_new = jnp.take(param, placing, axis=1)
    first_new = jnp.take(first, placing, axis=1)
    second_new = jnp.take(second, placing, axis=1)
    weights = param.astype(jnp.bfloat16)
    return (param_new, first_new, second_new, weights)
```

```python
import jax
import jax.numpy as jnp
from jax import lax
from jax.experimental import pallas as pl
from jax.experimental.pallas import tpu as pltpu
from jax.sharding import Mesh, PartitionSpec as P

KV = 4
HD = 128
GRP = 8
STEP = 1000
LOG2E = 1.4426950408889634
MIB = 1 << 20

beta_first = 0.9
beta_second = 0.95
learning_rate = 0.02
decay_rate = 0.1
epsilon = 1e-08

PLANE = 512
CHUNK = 256
WHOLE = pl.BlockSpec(memory_space=pltpu.VMEM)
SCALARS = pl.BlockSpec(memory_space=pltpu.SMEM)
NT = (((1,), (1,)), ((), ()))
TN = (((0,), (0,)), ((), ()))


def swapped(x, axes):
    return lax.all_to_all(x, axes, split_axis=0, concat_axis=0, tiled=True)


def from_everyone(x, axes):
    return swapped(jnp.broadcast_to(x, (lax.axis_size(axes), *x.shape)), axes)


def value_kernel(place, q_ref, k_ref, d_ref, out_ref, own_ref, s_a, s_b, total):
    plane = place[0]
    factor = HD**-0.5 * LOG2E

    def scores(h, last, s_ref):
        q = q_ref[:, pl.ds(pl.multiple_of(h * HD, HD), HD)]
        top = jnp.full((8, PLANE), -jnp.inf, jnp.float32)
        for at in range(0, (last + 1) * PLANE, CHUNK):
            s = lax.dot_general(k_ref[at : at + CHUNK, :], q, NT, preferred_element_type=jnp.float32)
            if at >= last * PLANE:
                key = lax.broadcasted_iota(jnp.int32, s.shape, 0) + (at - last * PLANE)
                s = jnp.where(key <= lax.broadcasted_iota(jnp.int32, s.shape, 1), s, -jnp.inf)
            s_ref[at : at + CHUNK, :] = s
            top = jnp.maximum(top, jnp.max(s.reshape(CHUNK // 8, 8, PLANE), axis=0))
        return jnp.max(top, axis=0, keepdims=True)

    def add_terms(h, last, s_ref, top):
        d = d_ref[:, pl.ds(pl.multiple_of(h * HD, HD), HD)]
        size = jnp.zeros((8, PLANE), jnp.float32)
        for at in range(0, (last + 1) * PLANE, CHUNK):
            w = jnp.exp2((s_ref[at : at + CHUNK, :] - top) * factor)
            s_ref[at : at + CHUNK, :] = w
            size = size + jnp.sum(w.reshape(CHUNK // 8, 8, PLANE), axis=0)
        inverse = 1.0 / jnp.sum(size, axis=0, keepdims=True)
        for at in range(0, (last + 1) * PLANE, CHUNK):
            p = (s_ref[at : at + CHUNK, :] * inverse).astype(jnp.bfloat16)
            total[at : at + CHUNK, :] += jnp.dot(p, d, preferred_element_type=jnp.float32)

    for last in range(4):

        @pl.when(plane == last)
        def _(last=last):
            total[...] = jnp.zeros_like(total)

            @pl.loop(0, GRP // 2)
            def _(pair):
                top_a = scores(2 * pair, last, s_a)
                top_b = scores(2 * pair + 1, last, s_b)
                add_terms(2 * pair, last, s_a, top_a)
                add_terms(2 * pair + 1, last, s_b, top_b)

            own_ref[...] = total[last * PLANE : (last + 1) * PLANE, :]
            for k in range(4):
                out_ref[k] = total[k * PLANE : (k + 1) * PLANE, :].astype(jnp.bfloat16)


def value_terms(place, q, k, d):
    return pl.pallas_call(
        value_kernel,
        out_shape=(
            jax.ShapeDtypeStruct((4, PLANE, HD), jnp.bfloat16),
            jax.ShapeDtypeStruct((PLANE, HD), jnp.float32),
        ),
        in_specs=[SCALARS, WHOLE, WHOLE, WHOLE],
        out_specs=(WHOLE, WHOLE),
        scratch_shapes=[
            pltpu.VMEM((4 * PLANE, PLANE), jnp.float32),
            pltpu.VMEM((4 * PLANE, PLANE), jnp.float32),
            pltpu.VMEM((4 * PLANE, HD), jnp.float32),
        ],
        compiler_params=pltpu.CompilerParams(vmem_limit_bytes=40 * MIB),
        cost_estimate=pl.CostEstimate(flops=12 * 10**9, bytes_accessed=4 * MIB, transcendentals=8 * 10**6),
        name="values",
    )(place, q, k, d)


def gradient_kernel(place, in_ref, v_ref, out_ref, own_ref, values, rows):
    y = place[0]
    for c in range(2):
        for g in range(KV):
            values[c * PLANE : (c + 1) * PLANE, g * HD : (g + 1) * HD] = v_ref[c * KV + g]

    @pl.loop(0, 8)
    def _(b):
        lhs = in_ref[:, pl.ds(pl.multiple_of(b * 128, 128), 128)]
        rows[...] = lax.dot_general(lhs, values[...], TN, preferred_element_type=jnp.float32)
        for to in range(8):
            part = jnp.concatenate([rows[8 * to : 8 * to + 8, :], rows[64 + 8 * to : 72 + 8 * to, :]], axis=0)
            out_ref[to, b] = part.astype(jnp.bfloat16)
        mine = pl.multiple_of(8 * y, 8)
        own_ref[b, 0:8, :] = rows[pl.ds(mine, 8), :]
        own_ref[b, 8:16, :] = rows[pl.ds(mine + 64, 8), :]


def gradient_terms(place, pieces, values):
    return pl.pallas_call(
        gradient_kernel,
        out_shape=(
            jax.ShapeDtypeStruct((8, 8, 16, KV * HD), jnp.bfloat16),
            jax.ShapeDtypeStruct((8, 16, KV * HD), jnp.float32),
        ),
        in_specs=[SCALARS, WHOLE, WHOLE],
        out_specs=(WHOLE, WHOLE),
        scratch_shapes=[
            pltpu.VMEM((2 * PLANE, KV * HD), jnp.bfloat16),
            pltpu.VMEM((128, KV * HD), jnp.float32),
        ],
        compiler_params=pltpu.CompilerParams(vmem_limit_bytes=32 * MIB),
        cost_estimate=pl.CostEstimate(flops=2 * 10**9, bytes_accessed=4 * MIB, transcendentals=0),
        name="gradient",
    )(place, pieces, values)


def update_kernel(
    place, old_owner, new_owner, g_ref, st_ref, p_out, f_out, s_out, w_out, w_rows, old_count, new_count
):
    me = place[0]
    for i in range(16):
        old_count[i] = 0
        new_count[i] = 0

    @pl.loop(0, 64)
    def _(b):
        old = old_owner[b]
        slot = old_count[old]
        old_count[old] = slot + 1
        new = new_owner[b]
        to = new_count[new]
        new_count[new] = to + 1
        owner = (b // 32) * 16 + ((b // 2) % 4) * 4 + (b // 8) % 4
        gradient = g_ref[owner, b % 2]
        param = st_ref[old % 4, old // 4, 0, slot]
        first = beta_first * st_ref[old % 4, old // 4, 1, slot] + (1.0 - beta_first) * gradient
        second = beta_second * st_ref[old % 4, old // 4, 2, slot] + (1.0 - beta_second) * gradient * gradient
        first_hat = first / (1.0 - beta_first**STEP)
        second_hat = second / (1.0 - beta_second**STEP)
        param = param - learning_rate * (first_hat / (jnp.sqrt(second_hat) + epsilon) + decay_rate * param)
        for i in range(4):
            w_rows[i, pl.ds(b, 1), :] = param[i : i + 1, :]

        @pl.when(new == me)
        def _():
            p_out[to] = param
            f_out[to] = first
            s_out[to] = second

    w_out[...] = w_rows[...].astype(jnp.bfloat16)


def updated(place, old_owner, new_owner, gradient, state):
    block = jax.ShapeDtypeStruct((4, 4, KV * HD), jnp.float32)
    return pl.pallas_call(
        update_kernel,
        out_shape=(block, block, block, jax.ShapeDtypeStruct((4, 64, KV * HD), jnp.bfloat16)),
        in_specs=[SCALARS, SCALARS, SCALARS, WHOLE, WHOLE],
        out_specs=(WHOLE,) * 4,
        scratch_shapes=[
            pltpu.VMEM((4, 64, KV * HD), jnp.float32),
            pltpu.SMEM((16,), jnp.int32),
            pltpu.SMEM((16,), jnp.int32),
        ],
        compiler_params=pltpu.CompilerParams(vmem_limit_bytes=32 * MIB),
        cost_estimate=pl.CostEstimate(flops=4 * 10**6, bytes_accessed=4 * MIB, transcendentals=3 * 10**5),
        name="update",
    )(place, old_owner, new_owner, gradient, state)


def local(queries, keys, grad_out, inputs, old_owner, new_owner, param_old, first_old, second_old):
    here = queries.shape[0]
    zl = lax.axis_index("zl")
    y = lax.axis_index("y")
    shard = zl * 4 + lax.axis_index("x")

    by_group = keys.reshape(here, KV, HD).transpose(1, 0, 2)
    keys_all = swapped(jnp.broadcast_to(by_group, (4, KV, here, HD)).reshape(16, here, HD), ("zl", "x"))
    keys_all = keys_all.reshape(4 * PLANE, HD)
    q = swapped(queries.reshape(here, KV, GRP * HD).transpose(1, 0, 2), "x").reshape(PLANE, GRP * HD)
    d = swapped(grad_out.reshape(here, KV, GRP * HD).transpose(1, 0, 2), "x").reshape(PLANE, GRP * HD)
    pieces = swapped(inputs.reshape(here, 8, 1024).transpose(1, 0, 2), ("c", "x")).reshape(2 * PLANE, 1024)

    state = jnp.stack([a.transpose(1, 0, 2) for a in (param_old, first_old, second_old)])
    state = from_everyone(from_everyone(state, "zl"), "x")

    parts, own = value_terms(zl.reshape(1).astype(jnp.int32), q, keys_all, d)
    arrived = swapped(parts, "zl").astype(jnp.float32)
    source = jnp.arange(4)[:, None, None]
    values = (own + jnp.sum(jnp.where(source == zl, 0.0, arrived), axis=0)).astype(jnp.bfloat16)
    values = from_everyone(values, ("c", "x"))

    parts, own = gradient_terms(y.reshape(1).astype(jnp.int32), pieces, values)
    arrived = swapped(parts, "y").astype(jnp.float32)
    source = jnp.arange(8)[:, None, None, None]
    rows = own + jnp.sum(jnp.where(source == y, 0.0, arrived), axis=0)
    rows = rows.reshape(4, 2, 2, 8, KV * HD).transpose(2, 0, 1, 3, 4).reshape(8, 2, 8, KV * HD)
    rows = jnp.sum(swapped(rows, ("zh", "zl")), axis=0)
    by_core = rows.reshape(2, 2, 4, KV * HD).transpose(1, 0, 2, 3)
    by_core = jnp.broadcast_to(by_core[:, None], (2, 16, 2, 4, KV * HD)).reshape(32, 2, 4, KV * HD)
    gradient = swapped(by_core, ("c", "zl", "x"))

    *states, weights = updated(shard.reshape(1).astype(jnp.int32), old_owner, new_owner, gradient, state)
    return (*(a.transpose(1, 0, 2) for a in states), weights)


def solution(mesh):
    fine = Mesh(mesh.devices.reshape(2, 8, 2, 4, 4), ("zh", "y", "c", "zl", "x"))
    rep = ("zh", "y", "c")
    shard = ("zl", "x")
    tokens = P((*rep, *shard), None)
    placed = (tokens,) * 4 + (P(), P()) + (P(rep, shard, None),) * 3
    return jax.shard_map(
        local,
        mesh=fine,
        in_specs=placed,
        out_specs=(P(rep, shard, None),) * 3 + (P(rep, None, None),),
        check_vma=False,
    )
```

```python
import functools

import jax
import jax.numpy as jnp
from jax import lax
from jax.experimental import pallas as pl
from jax.experimental.pallas import tpu as pltpu
from jax.sharding import Mesh, PartitionSpec as P

KV = 4
HD = 128
GRP = 8
STEP = 1000
LOG2E = 1.4426950408889634
MIB = 1 << 20

beta_first = 0.9
beta_second = 0.95
learning_rate = 0.02
decay_rate = 0.1
epsilon = 1e-08

PLANE = 512
CHUNK = 256
ZH, Y, C, ZL, X = range(5)
WHOLE = pl.BlockSpec(memory_space=pltpu.VMEM)
SCALARS = pl.BlockSpec(memory_space=pltpu.SMEM)
NT = (((1,), (1,)), ((), ()))
TN = (((0,), (0,)), ((), ()))


def swapped(x, axes):
    return lax.all_to_all(x, axes, split_axis=0, concat_axis=0, tiled=True)


def shifted(x, axis, k):
    n = lax.axis_size(axis)
    return lax.ppermute(x, axis, [(i, (i + k) % n) for i in range(n)])


def around(own, axis, parts=None):
    return [own] + [shifted(own if parts is None else parts[k - 1], axis, k) for k in (1, 2, 3)]


def after(x, *done):
    return lax.optimization_barrier((x, *done))[0]


def call(kernel, name, out, scalars, arrays, scratch, flops=10**6, moved=4 * MIB, special=0, limit=40):
    return pl.pallas_call(
        kernel,
        out_shape=out,
        in_specs=[SCALARS] * len(scalars) + [WHOLE] * len(arrays),
        out_specs=jax.tree.map(lambda _: WHOLE, out),
        scratch_shapes=scratch,
        compiler_params=pltpu.CompilerParams(vmem_limit_bytes=limit * MIB),
        cost_estimate=pl.CostEstimate(flops=flops, bytes_accessed=moved, transcendentals=special),
        name=name,
    )(*scalars, *arrays)


def shape(*dims, dtype=jnp.bfloat16):
    return jax.ShapeDtypeStruct(dims, dtype)


def pack_heads_kernel(place, q_ref, d_ref, *out):
    for half in range(2):
        for k in range(4):
            at = ((place[X] + k) % 4) * GRP * HD + half * 512
            at = pl.ds(pl.multiple_of(at, 512), 512)
            out[4 * half + k][:, 0:512] = q_ref[:, at]
            out[4 * half + k][:, 512:1024] = d_ref[:, at]


def pack_inputs_kernel(place, in_ref, kept, sent):
    for k in range(4):
        at = ((place[X] + k) % 4) * 2048
        for c, out in ((place[C], kept), (1 - place[C], sent)):
            out[k] = in_ref[:, pl.ds(pl.multiple_of(at + c * 1024, 1024), 1024)]


def value_kernel(half, place, k_ref, r0, r1, r2, r3, *refs):
    plane = place[ZL]
    factor = HD**-0.5 * LOG2E
    if half == 0:
        total, q_ref, d_ref, s_a, s_b = refs
    else:
        before, out_ref, own_ref, q_ref, d_ref, s_a, s_b, total = refs
    for k, part in enumerate((r0, r1, r2, r3)):
        rows = pl.ds(pl.multiple_of(((place[X] + 4 - k) % 4) * 128, 128), 128)
        q_ref[rows, :] = part[:, 0:512]
        d_ref[rows, :] = part[:, 512:1024]

    def scores(h, last, s_ref):
        q = q_ref[:, pl.ds(pl.multiple_of(h * HD, HD), HD)]
        top = jnp.full((8, PLANE), -jnp.inf, jnp.float32)
        for at in range(0, (last + 1) * PLANE, CHUNK):
            s = lax.dot_general(k_ref[at : at + CHUNK, :], q, NT, preferred_element_type=jnp.float32)
            if at >= last * PLANE:
                key = lax.broadcasted_iota(jnp.int32, s.shape, 0) + (at - last * PLANE)
                s = jnp.where(key <= lax.broadcasted_iota(jnp.int32, s.shape, 1), s, -jnp.inf)
            s_ref[at : at + CHUNK, :] = s
            top = jnp.maximum(top, jnp.max(s.reshape(CHUNK // 8, 8, PLANE), axis=0))
        return jnp.max(top, axis=0, keepdims=True)

    def add_terms(h, last, s_ref, top):
        d = d_ref[:, pl.ds(pl.multiple_of(h * HD, HD), HD)]
        size = jnp.zeros((8, PLANE), jnp.float32)
        for at in range(0, (last + 1) * PLANE, CHUNK):
            w = jnp.exp2((s_ref[at : at + CHUNK, :] - top) * factor)
            s_ref[at : at + CHUNK, :] = w
            size = size + jnp.sum(w.reshape(CHUNK // 8, 8, PLANE), axis=0)
        inverse = 1.0 / jnp.sum(size, axis=0, keepdims=True)
        for at in range(0, (last + 1) * PLANE, CHUNK):
            p = (s_ref[at : at + CHUNK, :] * inverse).astype(jnp.bfloat16)
            total[at : at + CHUNK, :] += jnp.dot(p, d, preferred_element_type=jnp.float32)

    for last in range(4):

        @pl.when(plane == last)
        def _(last=last):
            if half == 0:
                total[...] = jnp.zeros_like(total)
            else:
                total[...] = before[...]

            @pl.loop(0, GRP // 4)
            def _(pair):
                top_a = scores(2 * pair, last, s_a)
                top_b = scores(2 * pair + 1, last, s_b)
                add_terms(2 * pair, last, s_a, top_a)
                add_terms(2 * pair + 1, last, s_b, top_b)

            if half == 1:
                own_ref[...] = total[last * PLANE : (last + 1) * PLANE, :]
                for k in range(4):
                    out_ref[k] = total[k * PLANE : (k + 1) * PLANE, :].astype(jnp.bfloat16)


def value_terms(half, place, keys, parts, before=None):
    total = shape(4 * PLANE, HD, dtype=jnp.float32)
    own = shape(PLANE, HD, dtype=jnp.float32)
    scratch = [
        pltpu.VMEM((PLANE, 512), jnp.bfloat16),
        pltpu.VMEM((PLANE, 512), jnp.bfloat16),
        pltpu.VMEM((4 * PLANE, PLANE), jnp.float32),
        pltpu.VMEM((4 * PLANE, PLANE), jnp.float32),
    ]
    return call(
        functools.partial(value_kernel, half),
        "values",
        total if half == 0 else (shape(4, PLANE, HD), own),
        [place],
        [keys, *parts, *([] if half == 0 else [before])],
        scratch if half == 0 else [*scratch, pltpu.VMEM((4 * PLANE, HD), jnp.float32)],
        flops=6 * 10**9,
        special=4 * 10**6,
    )


def sum_values_kernel(place, in_ref, own_ref, out_ref):
    total = own_ref[...] - in_ref[place[ZL]].astype(jnp.float32)
    for k in range(4):
        total = total + in_ref[k].astype(jnp.float32)
    rounded = total.astype(jnp.bfloat16)
    for k in range(8):
        out_ref[k] = rounded


def gradient_kernel(place, i0, i1, i2, i3, v_ref, out_ref, own_ref, values, rows_a, rows_b):
    for k in range(4):
        source = pl.ds(pl.multiple_of(((place[X] + 4 - k) % 4) * 128, 128), 128)
        for other in range(2):
            core = place[C] if other == 0 else 1 - place[C]
            at = (2 * k + other) * 128
            for g in range(KV):
                values[at : at + 128, g * HD : (g + 1) * HD] = v_ref[core * KV + g, source, :]

    @pl.loop(0, 4)
    def _(zl):
        for half, rows in enumerate((rows_a, rows_b)):
            at = pl.ds(pl.multiple_of(zl * 256 + half * 128, 128), 128)
            total = None
            for k, in_ref in enumerate((i0, i1, i2, i3)):
                term = lax.dot_general(
                    in_ref[:, at], values[256 * k : 256 * k + 256, :], TN, preferred_element_type=jnp.float32
                )
                total = term if total is None else total + term
            rows[...] = total
        for to in range(16):
            part = jnp.concatenate([rows_a[8 * to : 8 * to + 8, :], rows_b[8 * to : 8 * to + 8, :]], axis=0)
            out_ref[to * 4 + zl] = part.astype(jnp.bfloat16)

        @pl.when(zl == place[ZL])
        def _():
            mine = pl.ds(pl.multiple_of((place[ZH] * 8 + place[Y]) * 8, 8), 8)
            own_ref[0:8, :] = rows_a[mine, :]
            own_ref[8:16, :] = rows_b[mine, :]


def sum_rows_kernel(place, in_ref, own_ref, out_ref):
    total = own_ref[...] - in_ref[place[ZH] * 32 + place[Y] * 4 + place[ZL]].astype(jnp.float32)
    for k in range(64):
        total = total + in_ref[k].astype(jnp.float32)
    for c in range(2):
        for half in range(2):
            part = total[half * 8 + c * 4 : half * 8 + c * 4 + 4, :]
            for k in range(16):
                out_ref[16 * c + k, half] = part


def order_kernel(place, old_owner, s0, s1, s2, s3, out_ref, count):
    for i in range(16):
        count[i] = 0

    @pl.loop(0, 64)
    def _(b):
        old = old_owner[b]
        slot = count[old]
        count[old] = slot + 1
        kz = (place[ZL] + 4 - old // 4) % 4
        kx = (place[X] + 4 - old % 4) % 4
        for k, s_ref in enumerate((s0, s1, s2, s3)):

            @pl.when(kx == k)
            def _(s_ref=s_ref):
                for part in range(3):
                    out_ref[b, part] = s_ref[kz, part, slot]


def update_kernel(place, new_owner, g_ref, st_ref, p_out, f_out, s_out, w_out, w_rows, changed, count):
    @pl.loop(0, 64, unroll=4)
    def _(b):
        owner = ((b // 8) % 2) * 16 + ((b // 2) % 4) * 4 + b // 16
        gradient = g_ref[owner, b % 2]
        param = st_ref[b, 0]
        first = beta_first * st_ref[b, 1] + (1.0 - beta_first) * gradient
        second = beta_second * st_ref[b, 2] + (1.0 - beta_second) * gradient * gradient
        first_hat = first / (1.0 - beta_first**STEP)
        second_hat = second / (1.0 - beta_second**STEP)
        param = param - learning_rate * (first_hat / (jnp.sqrt(second_hat) + epsilon) + decay_rate * param)
        for i in range(4):
            w_rows[i, pl.ds(b, 1), :] = param[i : i + 1, :]
        changed[b, 0] = param
        changed[b, 1] = first
        changed[b, 2] = second

    w_out[...] = w_rows[...].astype(jnp.bfloat16)
    count[0] = 0

    @pl.loop(0, 64)
    def _(b):
        @pl.when(new_owner[b] == place[ZL] * 4 + place[X])
        def _():
            to = count[0]
            count[0] = to + 1
            for part, out in enumerate((p_out, f_out, s_out)):
                block = changed[b, part]
                for i in range(4):
                    out[i, pl.ds(to, 1), :] = block[i : i + 1, :]


def local(queries, keys, grad_out, inputs, old_owner, new_owner, param_old, first_old, second_old):
    f32 = jnp.float32
    here = queries.shape[0]
    place = jnp.stack([lax.axis_index(a) for a in ("zh", "y", "c", "zl", "x")]).astype(jnp.int32)

    by_group = keys.reshape(here, KV, HD).transpose(1, 0, 2)
    keys_all = swapped(jnp.broadcast_to(by_group, (4, KV, here, HD)).reshape(16, here, HD), ("zl", "x"))
    keys_all = keys_all.reshape(4 * PLANE, HD)
    packed = call(
        pack_heads_kernel, "pack_heads", (shape(here, 1024),) * 8, [place], [queries, grad_out], []
    )
    early = around(packed[0], "x", packed[1:4])
    late = around(packed[4], "x", packed[5:8])
    kept, sent = call(
        pack_inputs_kernel, "pack_inputs", (shape(4, here, 1024),) * 2, [place], [inputs], []
    )
    other = shifted(sent, "c", 1)

    total = value_terms(0, place, keys_all, early)
    kept, other, total = lax.optimization_barrier((kept, other, total))
    pieces = [jnp.concatenate([kept[k], other[k]], axis=0) for k in range(4)]
    pieces = around(pieces[0], "x", pieces[1:])
    parts, own = value_terms(1, place, keys_all, late, total)
    arrived = swapped(parts, "zl")
    values = call(sum_values_kernel, "sum_values", shape(8, PLANE, HD), [place], [arrived, own], [])

    state = jnp.stack([a.transpose(1, 0, 2) for a in (param_old, first_old, second_old)])
    state = jnp.stack(around(after(state, values), "zl"))
    values, pieces = lax.optimization_barrier((values, pieces))
    values = swapped(values, ("c", "x"))

    parts, own = call(
        gradient_kernel,
        "gradient",
        (shape(64, 16, KV * HD), shape(16, KV * HD, dtype=f32)),
        [place],
        [*pieces, values],
        [pltpu.VMEM((2 * PLANE, KV * HD), jnp.bfloat16)] + [pltpu.VMEM((128, KV * HD), f32)] * 2,
        flops=2 * 10**9,
    )
    state, parts = lax.optimization_barrier((state, parts))
    arrived = swapped(parts, ("zh", "y", "zl"))
    state = around(state, "x")
    state = call(
        order_kernel,
        "order",
        shape(64, 3, 4, KV * HD, dtype=f32),
        [place, old_owner],
        state,
        [pltpu.SMEM((16,), jnp.int32)],
    )
    rows = call(sum_rows_kernel, "sum_rows", shape(32, 2, 4, KV * HD, dtype=f32), [place], [arrived, own], [])
    rows, state = lax.optimization_barrier((rows, state))
    gradient = swapped(rows, ("c", "zl", "x"))
    block = shape(4, 4, KV * HD, dtype=f32)
    return call(
        update_kernel,
        "update",
        (block, block, block, shape(4, 64, KV * HD)),
        [place, new_owner],
        [gradient, state],
        [
            pltpu.VMEM((4, 64, KV * HD), f32),
            pltpu.VMEM((64, 3, 4, KV * HD), f32),
            pltpu.SMEM((1,), jnp.int32),
        ],
    )


def solution(mesh):
    fine = Mesh(mesh.devices.reshape(2, 8, 2, 4, 4), ("zh", "y", "c", "zl", "x"))
    rep = ("zh", "y", "c")
    shard = ("zl", "x")
    tokens = P((*rep, *shard), None)
    placed = (tokens,) * 4 + (P(), P()) + (P(rep, shard, None),) * 3
    return jax.shard_map(
        local,
        mesh=fine,
        in_specs=placed,
        out_specs=(P(rep, shard, None),) * 3 + (P(rep, None, None),),
        check_vma=False,
    )
```

```python
import functools

import jax
import jax.numpy as jnp
from jax import lax
from jax.experimental import pallas as pl
from jax.experimental.pallas import tpu as pltpu
from jax.sharding import Mesh, PartitionSpec as P

KV = 4
HD = 128
GRP = 8
STEP = 1000
LOG2E = 1.4426950408889634
MIB = 1 << 20

beta_first = 0.9
beta_second = 0.95
learning_rate = 0.02
decay_rate = 0.1
epsilon = 1e-08

PLANE = 512
CHUNK = 256
QUERIES = 256
FIRST, SECOND = (0, 1), (3, 2)
ZH, Y, C, ZL, X = range(5)
WHOLE = pl.BlockSpec(memory_space=pltpu.VMEM)
ELSEWHERE = pl.BlockSpec(memory_space=pl.ANY)
SCALARS = pl.BlockSpec(memory_space=pltpu.SMEM)
NT = (((1,), (1,)), ((), ()))
TN = (((0,), (0,)), ((), ()))


def swapped(x, axes):
    return lax.all_to_all(x, axes, split_axis=0, concat_axis=0, tiled=True)


def shifted(x, axis, k):
    n = lax.axis_size(axis)
    return lax.ppermute(x, axis, [(i, (i + k) % n) for i in range(n)])


def sent_down(x, k):
    return lax.ppermute(x, "zl", [(i, i - k) for i in range(k, 4)])


def old_planes(x, k):
    return lax.ppermute(x, "zl", [(i, (i + k) % 4) for i in range(3)])


def call(kernel, name, out, scalars, arrays, scratch, behind=(), limit=20):
    given = len(scalars) + len(arrays)

    def body(*refs):
        kernel(*refs[:given], *refs[given + len(behind) :])

    return pl.pallas_call(
        body,
        out_shape=out,
        in_specs=[SCALARS] * len(scalars) + [WHOLE] * len(arrays) + [ELSEWHERE] * len(behind),
        out_specs=jax.tree.map(lambda _: WHOLE, out),
        scratch_shapes=scratch,
        compiler_params=pltpu.CompilerParams(vmem_limit_bytes=limit * MIB),
        cost_estimate=pl.CostEstimate(flops=1, bytes_accessed=1024, transcendentals=0),
        name=name,
    )(*scalars, *arrays, *behind)


def shape(*dims, dtype=jnp.bfloat16):
    return jax.ShapeDtypeStruct(dims, dtype)


def pack_keys_kernel(k_ref, out_ref):
    for g in range(KV):
        part = k_ref[:, g * HD : (g + 1) * HD]
        for zl in range(4):
            out_ref[zl * 4 + g] = part


def pack_heads_kernel(place, q_ref, d_ref, *out):
    for k in range(4):
        at = pl.ds(pl.multiple_of(((place[X] + k) % 4) * GRP * HD, GRP * HD), GRP * HD)
        out[k][:, 0 : GRP * HD] = q_ref[:, at]
        out[k][:, GRP * HD :] = d_ref[:, at]


def pack_inputs_kernel(in_ref, out_ref):
    for k in range(8):
        out_ref[k] = in_ref[:, k * 1024 : (k + 1) * 1024]


def stack_kernel(*refs):
    *parts, out_ref = refs
    for k, ref in enumerate(parts):
        out_ref[k] = ref[...]


def pack_states_kernel(place, *refs):
    *from_planes, out_ref = refs
    for k, ref in enumerate(from_planes):
        plane = (place[ZL] + 4 - k) % 4

        @pl.when(plane < 3)
        def _(ref=ref, plane=plane):
            out_ref[plane] = ref[...]


def value_kernel(steps, place, k_ref, ra, rb, *refs):
    plane = place[ZL]
    factor = HD**-0.5 * LOG2E
    if steps == FIRST:
        total, q_ref, d_ref, s_a, s_b = refs
    else:
        before, own_ref, *down, q_ref, d_ref, s_a, s_b, total = refs
    width = GRP * HD
    for at, part in ((0, ra), (128, rb)):
        q_ref[at : at + 128, :] = part[:, 0:width]
        d_ref[at : at + 128, :] = part[:, width:]
    starts = [((place[X] + 4 - k) % 4) * 128 for k in steps]
    column = lax.broadcasted_iota(jnp.int32, (CHUNK, QUERIES), 1)
    position = jnp.where(column < 128, column + starts[0], column - 128 + starts[1])
    ahead = position - lax.broadcasted_iota(jnp.int32, (CHUNK, QUERIES), 0)

    def scores(h, last, s_ref):
        q = q_ref[:, pl.ds(pl.multiple_of(h * HD, HD), HD)]
        top = jnp.full((8, QUERIES), -jnp.inf, jnp.float32)
        for at in range(0, (last + 1) * PLANE, CHUNK):
            s = lax.dot_general(k_ref[at : at + CHUNK, :], q, NT, preferred_element_type=jnp.float32)
            if at >= last * PLANE:
                s = jnp.where(ahead >= at - last * PLANE, s, -jnp.inf)
            s_ref[at : at + CHUNK, :] = s
            top = jnp.maximum(top, jnp.max(s.reshape(CHUNK // 8, 8, QUERIES), axis=0))
        return jnp.max(top, axis=0, keepdims=True)

    def add_terms(h, last, s_ref, top):
        d = d_ref[:, pl.ds(pl.multiple_of(h * HD, HD), HD)]
        size = jnp.zeros((8, QUERIES), jnp.float32)
        for at in range(0, (last + 1) * PLANE, CHUNK):
            w = jnp.exp2((s_ref[at : at + CHUNK, :] - top) * factor)
            s_ref[at : at + CHUNK, :] = w
            size = size + jnp.sum(w.reshape(CHUNK // 8, 8, QUERIES), axis=0)
        inverse = 1.0 / jnp.sum(size, axis=0, keepdims=True)
        for at in range(0, (last + 1) * PLANE, CHUNK):
            p = (s_ref[at : at + CHUNK, :] * inverse).astype(jnp.bfloat16)
            total[at : at + CHUNK, :] += jnp.dot(p, d, preferred_element_type=jnp.float32)

    for last in range(4):

        @pl.when(plane == last)
        def _(last=last):
            used = slice(0, (last + 1) * PLANE)
            if steps == FIRST:
                total[used, :] = jnp.zeros(((last + 1) * PLANE, HD), jnp.float32)
            else:
                total[used, :] = before[used, :]

            @pl.loop(0, GRP // 2)
            def _(pair):
                top_a = scores(2 * pair, last, s_a)
                top_b = scores(2 * pair + 1, last, s_b)
                add_terms(2 * pair, last, s_a, top_a)
                add_terms(2 * pair + 1, last, s_b, top_b)

            if steps != FIRST:
                own_ref[...] = total[last * PLANE : (last + 1) * PLANE, :]
                for k in range(1, last + 1):
                    down[k - 1][...] = total[(last - k) * PLANE : (last - k + 1) * PLANE, :].astype(jnp.bfloat16)


def value_terms(steps, place, keys, parts, before=None, behind=()):
    total = shape(4 * PLANE, HD, dtype=jnp.float32)
    own = shape(PLANE, HD, dtype=jnp.float32)
    scratch = [
        pltpu.VMEM((QUERIES, GRP * HD), jnp.bfloat16),
        pltpu.VMEM((QUERIES, GRP * HD), jnp.bfloat16),
        pltpu.VMEM((4 * PLANE, QUERIES), jnp.float32),
        pltpu.VMEM((4 * PLANE, QUERIES), jnp.float32),
    ]
    return call(
        functools.partial(value_kernel, steps),
        "values",
        total if steps == FIRST else (own, *(shape(PLANE, HD),) * 3),
        [place],
        [keys, *(parts[k] for k in steps), *([] if before is None else [before])],
        scratch if steps == FIRST else [*scratch, pltpu.VMEM((4 * PLANE, HD), jnp.float32)],
        behind,
    )


def sum_values_kernel(own_ref, a_ref, b_ref, c_ref, out_ref):
    total = own_ref[...]
    for ref in (a_ref, b_ref, c_ref):
        total = total + ref[...].astype(jnp.float32)
    rounded = total.astype(jnp.bfloat16)
    for k in range(8):
        out_ref[k] = rounded


def gradient_kernel(place, in_ref, v_ref, out_ref, own_ref, values, rows_a, rows_b):
    for c in range(2):
        for g in range(KV):
            values[c * PLANE : (c + 1) * PLANE, g * HD : (g + 1) * HD] = v_ref[c * KV + g]

    @pl.loop(0, 4)
    def _(zl):
        for half, rows in enumerate((rows_a, rows_b)):
            lhs = in_ref[:, pl.ds(pl.multiple_of(zl * 256 + half * 128, 128), 128)]
            rows[...] = lax.dot_general(lhs, values[...], TN, preferred_element_type=jnp.float32)
        for to in range(16):
            part = jnp.concatenate([rows_a[8 * to : 8 * to + 8, :], rows_b[8 * to : 8 * to + 8, :]], axis=0)
            out_ref[to * 4 + zl] = part.astype(jnp.bfloat16)

        @pl.when(zl == place[ZL])
        def _():
            mine = pl.ds(pl.multiple_of((place[ZH] * 8 + place[Y]) * 8, 8), 8)
            own_ref[0:8, :] = rows_a[mine, :]
            own_ref[8:16, :] = rows_b[mine, :]


def sum_rows_kernel(place, in_ref, own_ref, out_ref):
    total = own_ref[...] - in_ref[place[ZH] * 32 + place[Y] * 4 + place[ZL]].astype(jnp.float32)
    for k in range(64):
        total = total + in_ref[k].astype(jnp.float32)
    for c in range(2):
        for half in range(2):
            part = total[half * 8 + c * 4 : half * 8 + c * 4 + 4, :]
            for k in range(16):
                out_ref[16 * c + k, half] = part


def order_kernel(place, old_owner, s0, s1, s2, s3, out_ref, count):
    for i in range(16):
        count[i] = 0

    @pl.loop(0, 64)
    def _(b):
        old = old_owner[b]
        slot = count[old]
        count[old] = slot + 1
        kx = (place[X] + 4 - old % 4) % 4
        for k, s_ref in enumerate((s0, s1, s2, s3)):

            @pl.when(kx == k)
            def _(s_ref=s_ref):
                for part in range(3):
                    out_ref[b, part] = s_ref[old // 4, part, slot]


def update_kernel(place, new_owner, g_ref, st_ref, p_out, f_out, s_out, w_out, w_rows, changed, count):
    @pl.loop(0, 64, unroll=4)
    def _(b):
        owner = (b // 32) * 16 + ((b // 2) % 4) * 4 + (b // 8) % 4
        gradient = g_ref[owner, b % 2]
        param = st_ref[b, 0]
        first = beta_first * st_ref[b, 1] + (1.0 - beta_first) * gradient
        second = beta_second * st_ref[b, 2] + (1.0 - beta_second) * gradient * gradient
        first_hat = first / (1.0 - beta_first**STEP)
        second_hat = second / (1.0 - beta_second**STEP)
        param = param - learning_rate * (first_hat / (jnp.sqrt(second_hat) + epsilon) + decay_rate * param)
        for i in range(4):
            w_rows[i, pl.ds(b, 1), :] = param[i : i + 1, :]
        changed[b, 0] = param
        changed[b, 1] = first
        changed[b, 2] = second

    w_out[...] = w_rows[...].astype(jnp.bfloat16)
    count[0] = 0

    @pl.loop(0, 64)
    def _(b):
        @pl.when(new_owner[b] == place[ZL] * 4 + place[X])
        def _():
            to = count[0]
            count[0] = to + 1
            for part, out in enumerate((p_out, f_out, s_out)):
                block = changed[b, part]
                for i in range(4):
                    out[i, pl.ds(to, 1), :] = block[i : i + 1, :]


def local(queries, keys, grad_out, inputs, old_owner, new_owner, param_old, first_old, second_old):
    f32 = jnp.float32
    here = queries.shape[0]
    columns = KV * HD
    place = jnp.stack([lax.axis_index(a) for a in ("zh", "y", "c", "zl", "x")]).astype(jnp.int32)

    keys_all = call(pack_keys_kernel, "pack_keys", shape(16, here, HD), [], [keys], [])
    keys_all = swapped(keys_all, ("zl", "x")).reshape(4 * PLANE, HD)
    packed = call(
        pack_heads_kernel, "pack_heads", (shape(here, 2 * GRP * HD),) * 4, [place], [queries, grad_out], []
    )
    heads = {0: packed[0], **{k: shifted(packed[k], "x", k) for k in (1, 3, 2)}}
    total = value_terms(FIRST, place, keys_all, heads)
    late = [heads[2], heads[3], total]
    packed = call(pack_inputs_kernel, "pack_inputs", shape(8, here, 1024), [], [inputs], [], late)
    pieces = swapped(packed, ("c", "x"))
    own, *parts = value_terms(SECOND, place, keys_all, heads, total, [packed])
    parts = [sent_down(parts[k - 1], k) for k in (1, 2, 3)]
    values = call(sum_values_kernel, "sum_values", shape(8, PLANE, HD), [], [own, *parts], [], [pieces])
    state = [a.transpose(1, 0, 2) for a in (param_old, first_old, second_old)]
    state = call(stack_kernel, "stack", shape(3, *state[0].shape, dtype=f32), [], state, [], [values])
    planes = [state, *(old_planes(state, k) for k in (1, 2, 3))]
    values = swapped(values, ("c", "x"))
    state = call(
        pack_states_kernel, "pack_states", shape(3, *state.shape, dtype=f32), [place], planes, []
    )
    parts, own = call(
        gradient_kernel,
        "gradient",
        (shape(64, 16, columns), shape(16, columns, dtype=f32)),
        [place],
        [pieces.reshape(2 * PLANE, 1024), values],
        [pltpu.VMEM((2 * PLANE, columns), jnp.bfloat16)] + [pltpu.VMEM((128, columns), f32)] * 2,
        planes[1:],
    )
    arrived = swapped(parts, ("zh", "y", "zl"))
    state = [state, *(shifted(state, "x", k) for k in (1, 2, 3))]
    state = call(
        order_kernel,
        "order",
        shape(64, 3, 4, columns, dtype=f32),
        [place, old_owner],
        state,
        [pltpu.SMEM((16,), jnp.int32)],
    )
    rows = call(sum_rows_kernel, "sum_rows", shape(32, 2, 4, columns, dtype=f32), [place], [arrived, own], [], [state])
    gradient = swapped(rows, ("c", "zl", "x"))
    block = shape(4, 4, columns, dtype=f32)
    return call(
        update_kernel,
        "update",
        (block, block, block, shape(4, 64, columns)),
        [place, new_owner],
        [gradient, state],
        [
            pltpu.VMEM((4, 64, columns), f32),
            pltpu.VMEM((64, 3, 4, columns), f32),
            pltpu.SMEM((1,), jnp.int32),
        ],
    )


def solution(mesh):
    fine = Mesh(mesh.devices.reshape(2, 8, 2, 4, 4), ("zh", "y", "c", "zl", "x"))
    rep = ("zh", "y", "c")
    shard = ("zl", "x")
    tokens = P((*rep, *shard), None)
    placed = (tokens,) * 4 + (P(), P()) + (P(rep, shard, None),) * 3
    return jax.shard_map(
        local,
        mesh=fine,
        in_specs=placed,
        out_specs=(P(rep, shard, None),) * 3 + (P(rep, None, None),),
        check_vma=False,
    )
```

```python
import jax
import jax.numpy as jnp
from jax import lax
from jax.experimental import pallas as pl
from jax.experimental.pallas import tpu as pltpu
from jax.sharding import Mesh, PartitionSpec as P

KV = 4
HD = 128
GRP = 8
STEP = 1000
LOG2E = 1.4426950408889634
MIB = 1 << 20

beta_first = 0.9
beta_second = 0.95
learning_rate = 0.02
decay_rate = 0.1
epsilon = 1e-08

PLANE = 512
CHUNK = 256
ZH, Y, C, ZL, X = range(5)
WHOLE = pl.BlockSpec(memory_space=pltpu.VMEM)
IN_HBM = pl.BlockSpec(memory_space=pltpu.HBM)
ELSEWHERE = pl.BlockSpec(memory_space=pl.ANY)
SCALARS = pl.BlockSpec(memory_space=pltpu.SMEM)
NT = (((1,), (1,)), ((), ()))
TN = (((0,), (0,)), ((), ()))


def swapped(x, axes):
    return lax.all_to_all(x, axes, split_axis=0, concat_axis=0, tiled=True)


def shifted(x, axis, k):
    n = lax.axis_size(axis)
    return lax.ppermute(x, axis, [(i, (i + k) % n) for i in range(n)])


def sent_up(x, k):
    return lax.ppermute(x, "zl", [(i, i + k) for i in range(4 - k)])


def sent_down(x, k):
    return lax.ppermute(x, "zl", [(i, i - k) for i in range(k, 4)])


def old_planes(x, k):
    return lax.ppermute(x, "zl", [(i, (i + k) % 4) for i in range(3)])


def call(kernel, name, out, scalars, arrays, scratch, behind=(), limit=12):
    given = len(scalars) + len(arrays)

    def body(*refs):
        kernel(*refs[:given], *refs[given + len(behind) :])

    return pl.pallas_call(
        body,
        out_shape=out,
        in_specs=[SCALARS] * len(scalars) + [WHOLE] * len(arrays) + [ELSEWHERE] * len(behind),
        out_specs=jax.tree.map(lambda _: WHOLE, out),
        scratch_shapes=scratch,
        compiler_params=pltpu.CompilerParams(vmem_limit_bytes=limit * MIB),
        cost_estimate=pl.CostEstimate(flops=1, bytes_accessed=1024, transcendentals=0),
        name=name,
    )(*scalars, *arrays, *behind)


def gate(x, *behind):
    return pl.pallas_call(
        lambda *refs: None,
        out_shape=jax.ShapeDtypeStruct(x.shape, x.dtype),
        in_specs=[IN_HBM] + [ELSEWHERE] * len(behind),
        out_specs=IN_HBM,
        input_output_aliases={0: 0},
        compiler_params=pltpu.CompilerParams(vmem_limit_bytes=MIB),
        cost_estimate=pl.CostEstimate(flops=1, bytes_accessed=1024, transcendentals=0),
        name="gate",
    )(x, *behind)


def shape(*dims, dtype=jnp.bfloat16):
    return jax.ShapeDtypeStruct(dims, dtype)


def pack_keys_kernel(k_ref, out_ref):
    for g in range(KV):
        out_ref[g] = k_ref[:, g * HD : (g + 1) * HD]


def pack_heads_kernel(q_ref, d_ref, out_ref):
    width = GRP * HD
    for g in range(KV):
        out_ref[g, :, 0:width] = q_ref[:, g * width : (g + 1) * width]
        out_ref[g, :, width:] = d_ref[:, g * width : (g + 1) * width]


def pack_inputs_kernel(in_ref, out_ref):
    for k in range(8):
        out_ref[k] = in_ref[:, k * 1024 : (k + 1) * 1024]


def stack_kernel(*refs):
    *parts, out_ref = refs
    for k, ref in enumerate(parts):
        out_ref[k] = ref[...]


def pack_states_kernel(place, *refs):
    *from_planes, out_ref = refs
    for k, ref in enumerate(from_planes):
        plane = (place[ZL] + 4 - k) % 4

        @pl.when(plane < 3)
        def _(ref=ref, plane=plane):
            out_ref[plane] = ref[...]


def value_kernel(place, heads, k0, k1, k2, k3, own_ref, down1, down2, down3, s_a, s_b, total):
    plane = place[ZL]
    factor = HD**-0.5 * LOG2E
    width = GRP * HD

    def columns(start):
        at = pl.ds(pl.multiple_of(start, HD), HD)
        return heads[:, :, at].reshape(PLANE, HD)

    def scores(h, last, s_ref):
        q = columns(h * HD)
        top = jnp.full((8, PLANE), -jnp.inf, jnp.float32)
        for at in range(0, (last + 1) * PLANE, CHUNK):
            k_ref = (k0, k1, k2, k3)[last - at // PLANE]
            k = k_ref[at % PLANE : at % PLANE + CHUNK, :]
            s = lax.dot_general(k, q, NT, preferred_element_type=jnp.float32)
            if at >= last * PLANE:
                key = lax.broadcasted_iota(jnp.int32, s.shape, 0) + (at - last * PLANE)
                s = jnp.where(key <= lax.broadcasted_iota(jnp.int32, s.shape, 1), s, -jnp.inf)
            s_ref[at : at + CHUNK, :] = s
            top = jnp.maximum(top, jnp.max(s.reshape(CHUNK // 8, 8, PLANE), axis=0))
        return jnp.max(top, axis=0, keepdims=True)

    def add_terms(h, last, s_ref, top):
        d = columns(h * HD + width)
        size = jnp.zeros((8, PLANE), jnp.float32)
        for at in range(0, (last + 1) * PLANE, CHUNK):
            w = jnp.exp2((s_ref[at : at + CHUNK, :] - top) * factor)
            s_ref[at : at + CHUNK, :] = w
            size = size + jnp.sum(w.reshape(CHUNK // 8, 8, PLANE), axis=0)
        inverse = 1.0 / jnp.sum(size, axis=0, keepdims=True)
        for at in range(0, (last + 1) * PLANE, CHUNK):
            p = (s_ref[at : at + CHUNK, :] * inverse).astype(jnp.bfloat16)
            total[at : at + CHUNK, :] += jnp.dot(p, d, preferred_element_type=jnp.float32)

    for last in range(4):

        @pl.when(plane == last)
        def _(last=last):
            used = (last + 1) * PLANE
            total[0:used, :] = jnp.zeros((used, HD), jnp.float32)

            @pl.loop(0, GRP // 2)
            def _(pair):
                top_a = scores(2 * pair, last, s_a)
                top_b = scores(2 * pair + 1, last, s_b)
                add_terms(2 * pair, last, s_a, top_a)
                add_terms(2 * pair + 1, last, s_b, top_b)

            own_ref[...] = total[last * PLANE : used, :]
            for k, out in enumerate((down1, down2, down3)[:last], 1):
                out[...] = total[(last - k) * PLANE : (last - k + 1) * PLANE, :].astype(jnp.bfloat16)


def sum_values_kernel(own_ref, a_ref, b_ref, c_ref, out_ref):
    total = own_ref[...]
    for ref in (a_ref, b_ref, c_ref):
        total = total + ref[...].astype(jnp.float32)
    rounded = total.astype(jnp.bfloat16)
    for k in range(8):
        out_ref[k] = rounded


def gradient_kernel(place, in_ref, v_ref, out_ref, own_ref, values, rows_a, rows_b):
    for c in range(2):
        for g in range(KV):
            values[c * PLANE : (c + 1) * PLANE, g * HD : (g + 1) * HD] = v_ref[c * KV + g]

    @pl.loop(0, 4)
    def _(zl):
        for half, rows in enumerate((rows_a, rows_b)):
            lhs = in_ref[:, pl.ds(pl.multiple_of(zl * 256 + half * 128, 128), 128)]
            rows[...] = lax.dot_general(lhs, values[...], TN, preferred_element_type=jnp.float32)
        for to in range(16):
            part = jnp.concatenate([rows_a[8 * to : 8 * to + 8, :], rows_b[8 * to : 8 * to + 8, :]], axis=0)
            out_ref[to * 4 + zl] = part.astype(jnp.bfloat16)

        @pl.when(zl == place[ZL])
        def _():
            mine = pl.ds(pl.multiple_of((place[ZH] * 8 + place[Y]) * 8, 8), 8)
            own_ref[0:8, :] = rows_a[mine, :]
            own_ref[8:16, :] = rows_b[mine, :]


def sum_rows_kernel(place, in_ref, own_ref, out_ref):
    total = own_ref[...] - in_ref[place[ZH] * 32 + place[Y] * 4 + place[ZL]].astype(jnp.float32)
    for k in range(64):
        total = total + in_ref[k].astype(jnp.float32)
    for c in range(2):
        for half in range(2):
            part = total[half * 8 + c * 4 : half * 8 + c * 4 + 4, :]
            for k in range(16):
                out_ref[16 * c + k, half] = part


def order_kernel(place, old_owner, s0, s1, s2, s3, out_ref, count):
    for i in range(16):
        count[i] = 0

    @pl.loop(0, 64)
    def _(b):
        old = old_owner[b]
        slot = count[old]
        count[old] = slot + 1
        kx = (place[X] + 4 - old % 4) % 4
        for k, s_ref in enumerate((s0, s1, s2, s3)):

            @pl.when(kx == k)
            def _(s_ref=s_ref):
                for part in range(3):
                    out_ref[b, part] = s_ref[old // 4, part, slot]


def update_kernel(place, new_owner, g_ref, st_ref, p_out, f_out, s_out, w_out, w_rows, changed, count):
    @pl.loop(0, 64, unroll=4)
    def _(b):
        owner = (b // 32) * 16 + ((b // 2) % 4) * 4 + (b // 8) % 4
        gradient = g_ref[owner, b % 2]
        param = st_ref[b, 0]
        first = beta_first * st_ref[b, 1] + (1.0 - beta_first) * gradient
        second = beta_second * st_ref[b, 2] + (1.0 - beta_second) * gradient * gradient
        first_hat = first / (1.0 - beta_first**STEP)
        second_hat = second / (1.0 - beta_second**STEP)
        param = param - learning_rate * (first_hat / (jnp.sqrt(second_hat) + epsilon) + decay_rate * param)
        for i in range(4):
            w_rows[i, pl.ds(b, 1), :] = param[i : i + 1, :]
        changed[b, 0] = param
        changed[b, 1] = first
        changed[b, 2] = second

    w_out[...] = w_rows[...].astype(jnp.bfloat16)
    count[0] = 0

    @pl.loop(0, 64)
    def _(b):
        @pl.when(new_owner[b] == place[ZL] * 4 + place[X])
        def _():
            to = count[0]
            count[0] = to + 1
            for part, out in enumerate((p_out, f_out, s_out)):
                block = changed[b, part]
                for i in range(4):
                    out[i, pl.ds(to, 1), :] = block[i : i + 1, :]


def local(queries, keys, grad_out, inputs, old_owner, new_owner, param_old, first_old, second_old):
    f32 = jnp.float32
    here = queries.shape[0]
    columns = KV * HD
    place = jnp.stack([lax.axis_index(a) for a in ("zh", "y", "c", "zl", "x")]).astype(jnp.int32)

    packed = call(pack_keys_kernel, "pack_keys", shape(KV, here, HD), [], [keys], [])
    plane_keys = swapped(packed, "x").reshape(PLANE, HD)
    packed = call(
        pack_heads_kernel, "pack_heads", shape(KV, here, 2 * GRP * HD), [], [queries, grad_out], []
    )
    heads = swapped(gate(packed, plane_keys), "x")
    all_keys = [plane_keys, *(sent_up(plane_keys, k) for k in (1, 2, 3))]
    state = [a.transpose(1, 0, 2) for a in (param_old, first_old, second_old)]
    state = call(stack_kernel, "stack", shape(3, *state[0].shape, dtype=f32), [], state, [])
    planes = [state, *(old_planes(state, k) for k in (1, 2, 3))]
    packed = call(pack_inputs_kernel, "pack_inputs", shape(8, here, 1024), [], [inputs], [])
    pieces = swapped(gate(packed, heads, *all_keys[1:], *planes[1:]), ("c", "x"))

    own, *parts = call(
        value_kernel,
        "values",
        (shape(PLANE, HD, dtype=f32), *(shape(PLANE, HD),) * 3),
        [place],
        [heads, *all_keys],
        [pltpu.VMEM((4 * PLANE, PLANE), f32)] * 2 + [pltpu.VMEM((4 * PLANE, HD), f32)],
        limit=24,
    )
    parts = [sent_down(parts[k - 1], k) for k in (1, 2, 3)]
    values = call(sum_values_kernel, "sum_values", shape(8, PLANE, HD), [], [own, *parts], [], [pieces])
    packed = call(
        pack_states_kernel, "pack_states", shape(3, *state.shape, dtype=f32), [place], planes, [], [values]
    )
    values = swapped(values, ("c", "x"))
    state = [packed, *(shifted(packed, "x", k) for k in (1, 2, 3))]

    parts, own = call(
        gradient_kernel,
        "gradient",
        (shape(64, 16, columns), shape(16, columns, dtype=f32)),
        [place],
        [pieces.reshape(2 * PLANE, 1024), values],
        [pltpu.VMEM((2 * PLANE, columns), jnp.bfloat16)] + [pltpu.VMEM((128, columns), f32)] * 2,
        state[1:2],
    )
    arrived = swapped(parts, ("zh", "y", "zl"))
    state = call(
        order_kernel,
        "order",
        shape(64, 3, 4, columns, dtype=f32),
        [place, old_owner],
        state,
        [pltpu.SMEM((16,), jnp.int32)],
    )
    rows = call(sum_rows_kernel, "sum_rows", shape(32, 2, 4, columns, dtype=f32), [place], [arrived, own], [], [state])
    gradient = swapped(rows, ("c", "zl", "x"))
    block = shape(4, 4, columns, dtype=f32)
    return call(
        update_kernel,
        "update",
        (block, block, block, shape(4, 64, columns)),
        [place, new_owner],
        [gradient, state],
        [
            pltpu.VMEM((4, 64, columns), f32),
            pltpu.VMEM((64, 3, 4, columns), f32),
            pltpu.SMEM((1,), jnp.int32),
        ],
    )


def solution(mesh):
    fine = Mesh(mesh.devices.reshape(2, 8, 2, 4, 4), ("zh", "y", "c", "zl", "x"))
    rep = ("zh", "y", "c")
    shard = ("zl", "x")
    tokens = P((*rep, *shard), None)
    placed = (tokens,) * 4 + (P(), P()) + (P(rep, shard, None),) * 3
    return jax.shard_map(
        local,
        mesh=fine,
        in_specs=placed,
        out_specs=(P(rep, shard, None),) * 3 + (P(rep, None, None),),
        check_vma=False,
    )
```

```python
import functools

import jax
import jax.numpy as jnp
from jax import lax
from jax.experimental import pallas as pl
from jax.experimental.pallas import tpu as pltpu
from jax.sharding import Mesh, PartitionSpec as P

KV = 4
HD = 128
GRP = 8
STEP = 1000
LOG2E = 1.4426950408889634
MIB = 1 << 20

beta_first = 0.9
beta_second = 0.95
learning_rate = 0.02
decay_rate = 0.1
epsilon = 1e-08

PLANE = 512
CHUNK = 256
ZH, Y, C, ZL, X = range(5)
WHOLE = pl.BlockSpec(memory_space=pltpu.VMEM)
IN_HBM = pl.BlockSpec(memory_space=pltpu.HBM)
ELSEWHERE = pl.BlockSpec(memory_space=pl.ANY)
SCALARS = pl.BlockSpec(memory_space=pltpu.SMEM)
NT = (((1,), (1,)), ((), ()))
TN = (((0,), (0,)), ((), ()))


def swapped(x, axes):
    return lax.all_to_all(x, axes, split_axis=0, concat_axis=0, tiled=True)


def shifted(x, axis, k):
    n = lax.axis_size(axis)
    return lax.ppermute(x, axis, [(i, (i + k) % n) for i in range(n)])


def sent_up(x, k):
    return lax.ppermute(x, "zl", [(i, i + k) for i in range(4 - k)])


def sent_down(x, k):
    return lax.ppermute(x, "zl", [(i, i - k) for i in range(k, 4)])


def old_planes(x, k):
    return lax.ppermute(x, "zl", [(i, (i + k) % 4) for i in range(3)])


def call(kernel, name, out, scalars, arrays, scratch, behind=(), limit=8):
    given = len(scalars) + len(arrays)

    def body(*refs):
        kernel(*refs[:given], *refs[given + len(behind) :])

    return pl.pallas_call(
        body,
        out_shape=out,
        in_specs=[SCALARS] * len(scalars) + [WHOLE] * len(arrays) + [ELSEWHERE] * len(behind),
        out_specs=jax.tree.map(lambda _: WHOLE, out),
        scratch_shapes=scratch,
        compiler_params=pltpu.CompilerParams(vmem_limit_bytes=limit * MIB),
        cost_estimate=pl.CostEstimate(flops=1, bytes_accessed=1024, transcendentals=0),
        name=name,
    )(*scalars, *arrays, *behind)


def shape(*dims, dtype=jnp.bfloat16):
    return jax.ShapeDtypeStruct(dims, dtype)


def copy_all(pairs, done):
    copies = [pltpu.make_async_copy(a, b, done.at[i]) for i, (a, b) in enumerate(pairs)]
    for copy in copies:
        copy.start()
    for copy in copies:
        copy.wait()


def pack_heads_kernel(q_ref, d_ref, out_ref, done):
    width = GRP * HD
    pairs = []
    for g in range(KV):
        at = pl.ds(g * width, width)
        pairs.append((q_ref.at[:, at], out_ref.at[g, :, pl.ds(0, width)]))
        pairs.append((d_ref.at[:, at], out_ref.at[g, :, pl.ds(width, width)]))
    copy_all(pairs, done)


def pack_inputs_kernel(in_ref, out_ref, done):
    copy_all([(in_ref.at[:, pl.ds(k * 1024, 1024)], out_ref.at[k]) for k in range(8)], done)


def packed_in_hbm(kernel, name, out, arrays, limit, behind=()):
    given = len(arrays)

    def body(*refs):
        kernel(*refs[:given], *refs[given + len(behind) :])

    return pl.pallas_call(
        body,
        out_shape=out,
        in_specs=[IN_HBM] * given + [ELSEWHERE] * len(behind),
        out_specs=IN_HBM,
        scratch_shapes=[pltpu.SemaphoreType.DMA((8,))],
        compiler_params=pltpu.CompilerParams(vmem_limit_bytes=limit * MIB),
        cost_estimate=pl.CostEstimate(flops=1, bytes_accessed=1024, transcendentals=0),
        name=name,
    )(*arrays, *behind)


def pack_keys_kernel(place, k_ref, *out):
    for k, ref in enumerate(out):
        ref[...] = k_ref[:, pl.ds(pl.multiple_of(((place[X] + k) % 4) * HD, HD), HD)]


def join_keys_kernel(place, *refs):
    *parts, out_ref = refs
    for k, part in enumerate(parts):
        out_ref[pl.ds(pl.multiple_of(((place[X] + 4 - k) % 4) * 128, 128), 128), :] = part[...]


def pack_states_kernel(p_ref, f_ref, s_ref, out_ref):
    for slot in range(6):
        param = p_ref[slot]
        high = param.astype(jnp.bfloat16).astype(jnp.float32)
        rows = jnp.concatenate([high, param - high, f_ref[slot], s_ref[slot]], axis=0)
        out_ref[slot] = rows.astype(jnp.bfloat16)


def join_planes_kernel(place, *refs):
    *from_planes, out_ref = refs
    for k, ref in enumerate(from_planes):
        plane = (place[ZL] + 4 - k) % 4

        @pl.when(plane < 3)
        def _(ref=ref, plane=plane):
            out_ref[plane] = ref[...]


def value_kernel(place, heads, k0, k1, k2, k3, own_ref, down1, down2, down3, s_a, s_b, total):
    plane = place[ZL]
    factor = HD**-0.5 * LOG2E
    width = GRP * HD

    def columns(start):
        at = pl.ds(pl.multiple_of(start, HD), HD)
        return heads[:, :, at].reshape(PLANE, HD)

    def scores(h, last, s_ref):
        q = columns(h * HD)
        top = jnp.full((8, PLANE), -jnp.inf, jnp.float32)
        for at in range(0, (last + 1) * PLANE, CHUNK):
            k_ref = (k0, k1, k2, k3)[last - at // PLANE]
            k = k_ref[at % PLANE : at % PLANE + CHUNK, :]
            s = lax.dot_general(k, q, NT, preferred_element_type=jnp.float32)
            if at >= last * PLANE:
                key = lax.broadcasted_iota(jnp.int32, s.shape, 0) + (at - last * PLANE)
                s = jnp.where(key <= lax.broadcasted_iota(jnp.int32, s.shape, 1), s, -jnp.inf)
            s_ref[at : at + CHUNK, :] = s
            top = jnp.maximum(top, jnp.max(s.reshape(CHUNK // 8, 8, PLANE), axis=0))
        return jnp.max(top, axis=0, keepdims=True)

    def add_terms(h, last, s_ref, top):
        d = columns(h * HD + width)
        size = jnp.zeros((8, PLANE), jnp.float32)
        for at in range(0, (last + 1) * PLANE, CHUNK):
            w = jnp.exp2((s_ref[at : at + CHUNK, :] - top) * factor)
            s_ref[at : at + CHUNK, :] = w
            size = size + jnp.sum(w.reshape(CHUNK // 8, 8, PLANE), axis=0)
        inverse = 1.0 / jnp.sum(size, axis=0, keepdims=True)
        for at in range(0, (last + 1) * PLANE, CHUNK):
            p = (s_ref[at : at + CHUNK, :] * inverse).astype(jnp.bfloat16)
            total[at : at + CHUNK, :] += jnp.dot(p, d, preferred_element_type=jnp.float32)

    for last in range(4):

        @pl.when(plane == last)
        def _(last=last):
            used = (last + 1) * PLANE
            total[0:used, :] = jnp.zeros((used, HD), jnp.float32)

            @pl.loop(0, GRP // 2)
            def _(pair):
                top_a = scores(2 * pair, last, s_a)
                top_b = scores(2 * pair + 1, last, s_b)
                add_terms(2 * pair, last, s_a, top_a)
                add_terms(2 * pair + 1, last, s_b, top_b)

            own_ref[...] = total[last * PLANE : used, :]
            for k, out in enumerate((down1, down2, down3)[:last], 1):
                out[...] = total[(last - k) * PLANE : (last - k + 1) * PLANE, :].astype(jnp.bfloat16)


def sum_values_kernel(own_ref, a_ref, b_ref, c_ref, out_ref):
    total = own_ref[...]
    for ref in (a_ref, b_ref, c_ref):
        total = total + ref[...].astype(jnp.float32)
    rounded = total.astype(jnp.bfloat16)
    for k in range(8):
        out_ref[k] = rounded


def gradient_kernel(behind, place, in_ref, v_ref, *refs):
    out_ref, own_ref, values, rows_a, rows_b = refs[behind:]
    zl = pl.program_id(0)

    @pl.when(zl == 0)
    def _():
        for c in range(2):
            for g in range(KV):
                values[c * PLANE : (c + 1) * PLANE, g * HD : (g + 1) * HD] = v_ref[c * KV + g]

    for half, rows in enumerate((rows_a, rows_b)):
        lhs = in_ref[:, half * 128 : half * 128 + 128]
        rows[...] = lax.dot_general(lhs, values[...], TN, preferred_element_type=jnp.float32)
    for to in range(16):
        part = jnp.concatenate([rows_a[8 * to : 8 * to + 8, :], rows_b[8 * to : 8 * to + 8, :]], axis=0)
        out_ref[to, 0] = part.astype(jnp.bfloat16)

    @pl.when(zl == place[ZL])
    def _():
        mine = pl.ds(pl.multiple_of((place[ZH] * 8 + place[Y]) * 8, 8), 8)
        own_ref[0:8, :] = rows_a[mine, :]
        own_ref[8:16, :] = rows_b[mine, :]


def gradient_terms(place, pieces, values, behind):
    columns = KV * HD
    parts, own = pl.pallas_call(
        functools.partial(gradient_kernel, len(behind)),
        grid=(4,),
        out_shape=(shape(16, 4, 16, columns), shape(16, columns, dtype=jnp.float32)),
        in_specs=[
            SCALARS,
            pl.BlockSpec((2 * PLANE, 256), lambda i: (0, i)),
            pl.BlockSpec((8, PLANE, HD), lambda i: (0, 0, 0)),
            *[ELSEWHERE] * len(behind),
        ],
        out_specs=(
            pl.BlockSpec((16, 1, 16, columns), lambda i: (0, i, 0, 0)),
            pl.BlockSpec((16, columns), lambda i: (0, 0)),
        ),
        scratch_shapes=[pltpu.VMEM((2 * PLANE, columns), jnp.bfloat16)] + [pltpu.VMEM((128, columns), jnp.float32)] * 2,
        compiler_params=pltpu.CompilerParams(vmem_limit_bytes=8 * MIB),
        cost_estimate=pl.CostEstimate(flops=1, bytes_accessed=1024, transcendentals=0),
        name="gradient",
    )(place, pieces, values, *behind)
    return parts.reshape(64, 16, columns), own


def sum_rows_kernel(place, in_ref, own_ref, out_ref):
    total = own_ref[...] - in_ref[place[ZH] * 32 + place[Y] * 4 + place[ZL]].astype(jnp.float32)
    for k in range(64):
        total = total + in_ref[k].astype(jnp.float32)
    for c in range(2):
        for half in range(2):
            part = total[half * 8 + c * 4 : half * 8 + c * 4 + 4, :]
            for k in range(16):
                out_ref[16 * c + k, half] = part


def order_kernel(place, old_owner, s0, s1, s2, s3, out_ref, count):
    for i in range(16):
        count[i] = 0

    @pl.loop(0, 64)
    def _(b):
        old = old_owner[b]
        slot = count[old]
        count[old] = slot + 1
        kx = (place[X] + 4 - old % 4) % 4
        for k, s_ref in enumerate((s0, s1, s2, s3)):

            @pl.when(kx == k)
            def _(s_ref=s_ref):
                rows = s_ref[old // 4, slot].astype(jnp.float32)
                out_ref[b, 0] = rows[0:4, :] + rows[4:8, :]
                out_ref[b, 1] = rows[8:12, :]
                out_ref[b, 2] = rows[12:16, :]


def update_kernel(place, new_owner, g_ref, st_ref, p_out, f_out, s_out, w_out, w_rows, changed, count):
    @pl.loop(0, 64, unroll=4)
    def _(b):
        owner = (b // 32) * 16 + ((b // 2) % 4) * 4 + (b // 8) % 4
        gradient = g_ref[owner, b % 2]
        param = st_ref[b, 0]
        first = beta_first * st_ref[b, 1] + (1.0 - beta_first) * gradient
        second = beta_second * st_ref[b, 2] + (1.0 - beta_second) * gradient * gradient
        first_hat = first / (1.0 - beta_first**STEP)
        second_hat = second / (1.0 - beta_second**STEP)
        param = param - learning_rate * (first_hat / (jnp.sqrt(second_hat) + epsilon) + decay_rate * param)
        for i in range(4):
            w_rows[i, pl.ds(b, 1), :] = param[i : i + 1, :]
        changed[b, 0] = param
        changed[b, 1] = first
        changed[b, 2] = second

    w_out[...] = w_rows[...].astype(jnp.bfloat16)
    count[0] = 0

    @pl.loop(0, 64)
    def _(b):
        @pl.when(new_owner[b] == place[ZL] * 4 + place[X])
        def _():
            to = count[0]
            count[0] = to + 1
            for part, out in enumerate((p_out, f_out, s_out)):
                block = changed[b, part]
                for i in range(4):
                    out[i, pl.ds(to, 1), :] = block[i : i + 1, :]


def local(queries, keys, grad_out, inputs, old_owner, new_owner, param_old, first_old, second_old):
    f32 = jnp.float32
    here = queries.shape[0]
    columns = KV * HD
    place = jnp.stack([lax.axis_index(a) for a in ("zh", "y", "c", "zl", "x")]).astype(jnp.int32)

    packed = packed_in_hbm(
        pack_heads_kernel, "pack_heads", shape(KV, here, 2 * GRP * HD), [queries, grad_out], 60
    )
    heads = swapped(packed, "x")
    own, *packed = call(pack_keys_kernel, "pack_keys", (shape(here, HD),) * 4, [place], [keys], [])
    plane_keys = [own, *(shifted(packed[k - 1], "x", k) for k in (1, 2, 3))]
    plane_keys = call(join_keys_kernel, "join_keys", shape(PLANE, HD), [place], plane_keys, [])
    all_keys = [plane_keys, *(sent_up(plane_keys, k) for k in (1, 2, 3))]
    packed = packed_in_hbm(
        pack_inputs_kernel, "pack_inputs", shape(8, here, 1024), [inputs], 1, all_keys[1:]
    )
    pieces = swapped(packed, ("c", "x"))

    own, *parts = call(
        value_kernel,
        "values",
        (shape(PLANE, HD, dtype=f32), *(shape(PLANE, HD),) * 3),
        [place],
        [heads, *all_keys],
        [pltpu.VMEM((4 * PLANE, PLANE), f32)] * 2 + [pltpu.VMEM((4 * PLANE, HD), f32)],
        limit=16,
    )
    parts = [sent_down(parts[k - 1], k) for k in (1, 2, 3)]
    values = call(sum_values_kernel, "sum_values", shape(8, PLANE, HD), [], [own, *parts], [], [pieces])
    state = [a.transpose(1, 0, 2) for a in (param_old, first_old, second_old)]
    state = call(pack_states_kernel, "pack_states", shape(6, 16, columns), [], state, [], [values])
    planes = [state, *(old_planes(state, k) for k in (1, 2, 3))]
    values = swapped(values, ("c", "x"))

    parts, own = gradient_terms(place, pieces.reshape(2 * PLANE, 1024), values, planes[1:])
    state = call(join_planes_kernel, "join_planes", shape(3, 6, 16, columns), [place], planes, [])
    state = [state, *(shifted(state, "x", k) for k in (1, 2, 3))]
    arrived = swapped(parts, ("zh", "y", "zl"))
    rows = call(sum_rows_kernel, "sum_rows", shape(32, 2, 4, columns, dtype=f32), [place], [arrived, own], [], state[1:])
    state = call(
        order_kernel,
        "order",
        shape(64, 3, 4, columns, dtype=f32),
        [place, old_owner],
        state,
        [pltpu.SMEM((16,), jnp.int32)],
    )
    gradient = swapped(rows, ("c", "zl", "x"))
    block = shape(4, 4, columns, dtype=f32)
    return call(
        update_kernel,
        "update",
        (block, block, block, shape(4, 64, columns)),
        [place, new_owner],
        [gradient, state],
        [
            pltpu.VMEM((4, 64, columns), f32),
            pltpu.VMEM((64, 3, 4, columns), f32),
            pltpu.SMEM((1,), jnp.int32),
        ],
    )


def solution(mesh):
    fine = Mesh(mesh.devices.reshape(2, 8, 2, 4, 4), ("zh", "y", "c", "zl", "x"))
    rep = ("zh", "y", "c")
    shard = ("zl", "x")
    tokens = P((*rep, *shard), None)
    placed = (tokens,) * 4 + (P(), P()) + (P(rep, shard, None),) * 3
    return jax.shard_map(
        local,
        mesh=fine,
        in_specs=placed,
        out_specs=(P(rep, shard, None),) * 3 + (P(rep, None, None),),
        check_vma=False,
    )
```

```python
import functools

import jax
import jax.numpy as jnp
from jax import lax
from jax.experimental import pallas as pl
from jax.experimental.pallas import tpu as pltpu
from jax.sharding import Mesh, PartitionSpec as P

KV = 4
HD = 128
GRP = 8
STEP = 1000
LOG2E = 1.4426950408889634
MIB = 1 << 20

beta_first = 0.9
beta_second = 0.95
learning_rate = 0.02
decay_rate = 0.1
epsilon = 1e-08

PLANE = 512
CHUNK = 256
ZH, Y, C, ZL, X = range(5)
WHOLE = pl.BlockSpec(memory_space=pltpu.VMEM)
ELSEWHERE = pl.BlockSpec(memory_space=pl.ANY)
SCALARS = pl.BlockSpec(memory_space=pltpu.SMEM)
NT = (((1,), (1,)), ((), ()))
TN = (((0,), (0,)), ((), ()))


def swapped(x, axes):
    return lax.all_to_all(x, axes, split_axis=0, concat_axis=0, tiled=True)


def shifted(x, axis, k):
    n = lax.axis_size(axis)
    return lax.ppermute(x, axis, [(i, (i + k) % n) for i in range(n)])


def sent_up(x, k):
    return lax.ppermute(x, "zl", [(i, i + k) for i in range(4 - k)])


def sent_down(x, k):
    return lax.ppermute(x, "zl", [(i, i - k) for i in range(k, 4)])


def old_planes(x, k):
    return lax.ppermute(x, "zl", [(i, (i + k) % 4) for i in range(3)])


def call(kernel, name, out, scalars, arrays, scratch, behind=(), limit=8):
    given = len(scalars) + len(arrays)

    def body(*refs):
        kernel(*refs[:given], *refs[given + len(behind) :])

    return pl.pallas_call(
        body,
        out_shape=out,
        in_specs=[SCALARS] * len(scalars) + [WHOLE] * len(arrays) + [ELSEWHERE] * len(behind),
        out_specs=jax.tree.map(lambda _: WHOLE, out),
        scratch_shapes=scratch,
        compiler_params=pltpu.CompilerParams(vmem_limit_bytes=limit * MIB),
        cost_estimate=pl.CostEstimate(flops=1, bytes_accessed=1024, transcendentals=0),
        name=name,
    )(*scalars, *arrays, *behind)


def shape(*dims, dtype=jnp.bfloat16):
    return jax.ShapeDtypeStruct(dims, dtype)


def pack_heads_kernel(q_ref, d_ref, out_ref):
    width = GRP * HD
    for g in range(KV):
        out_ref[g, :, 0:width] = q_ref[:, g * width : (g + 1) * width]
        out_ref[g, :, width:] = d_ref[:, g * width : (g + 1) * width]


def pack_inputs_kernel(in_ref, out_ref):
    for k in range(8):
        out_ref[k] = in_ref[:, k * 1024 : (k + 1) * 1024]


def pack_keys_kernel(k_ref, out_ref):
    for g in range(KV):
        out_ref[g] = k_ref[:, g * HD : (g + 1) * HD]


def pack_states_kernel(p_ref, f_ref, s_ref, out_ref):
    for slot in range(6):
        param = p_ref[slot]
        high = param.astype(jnp.bfloat16).astype(jnp.float32)
        rows = jnp.concatenate([high, param - high, f_ref[slot], s_ref[slot]], axis=0)
        out_ref[slot] = rows.astype(jnp.bfloat16)


def join_planes_kernel(place, *refs):
    *from_planes, out_ref = refs
    for k, ref in enumerate(from_planes):
        plane = (place[ZL] + 4 - k) % 4

        @pl.when(plane < 3)
        def _(ref=ref, plane=plane):
            out_ref[plane] = ref[...]


def value_kernel(place, heads, k0, k1, k2, k3, own_ref, down1, down2, down3, s_a, s_b, total, tops):
    plane = place[ZL]
    factor = HD**-0.5 * LOG2E
    width = GRP * HD

    def columns(start):
        at = pl.ds(pl.multiple_of(start, HD), HD)
        return heads[:, :, at].reshape(PLANE, HD)

    def scores(q, at, last, s_ref, top):
        k_ref = (k0, k1, k2, k3)[last - at // PLANE]
        k = k_ref[at % PLANE : at % PLANE + CHUNK, :]
        s = lax.dot_general(k, q, NT, preferred_element_type=jnp.float32)
        if at >= last * PLANE:
            key = lax.broadcasted_iota(jnp.int32, s.shape, 0) + (at - last * PLANE)
            s = jnp.where(key <= lax.broadcasted_iota(jnp.int32, s.shape, 1), s, -jnp.inf)
        s_ref[at : at + CHUNK, :] = s
        return jnp.maximum(top, jnp.max(s.reshape(CHUNK // 8, 8, PLANE), axis=0))

    def powers(at, s_ref, top, size):
        w = jnp.exp2((s_ref[at : at + CHUNK, :] - top) * factor)
        s_ref[at : at + CHUNK, :] = w
        return size + jnp.sum(w.reshape(CHUNK // 8, 8, PLANE), axis=0)

    def add_terms(d, at, s_ref, inverse):
        p = (s_ref[at : at + CHUNK, :] * inverse).astype(jnp.bfloat16)
        total[at : at + CHUNK, :] += jnp.dot(p, d, preferred_element_type=jnp.float32)

    lowest = jnp.full((8, PLANE), -jnp.inf, jnp.float32)
    nothing = jnp.zeros((8, PLANE), jnp.float32)

    def largest(top):
        return jnp.max(top, axis=0, keepdims=True)

    def inverse_of(size):
        return 1.0 / jnp.sum(size, axis=0, keepdims=True)

    for last in range(4):

        @pl.when(plane == last)
        def _(last=last):
            used = (last + 1) * PLANE
            chunks = range(0, used, CHUNK)
            total[0:used, :] = jnp.zeros((used, HD), jnp.float32)
            top = lowest
            q = columns(0)
            for at in chunks:
                top = scores(q, at, last, s_a, top)
            tops[...] = largest(top)

            @pl.loop(0, GRP // 2)
            def _(pair):
                top_a = tops[...]
                q = columns((2 * pair + 1) * HD)
                top, size_a = lowest, nothing
                for at in chunks:
                    top = scores(q, at, last, s_b, top)
                    size_a = powers(at, s_a, top_a, size_a)
                top_b, inverse = largest(top), inverse_of(size_a)
                d = columns(2 * pair * HD + width)
                size_b = nothing
                for at in chunks:
                    add_terms(d, at, s_a, inverse)
                    size_b = powers(at, s_b, top_b, size_b)
                inverse = inverse_of(size_b)
                d = columns((2 * pair + 1) * HD + width)
                q = columns(jnp.minimum(2 * pair + 2, GRP - 1) * HD)
                top = lowest
                for at in chunks:
                    add_terms(d, at, s_b, inverse)
                    top = scores(q, at, last, s_a, top)
                tops[...] = largest(top)

            own_ref[...] = total[last * PLANE : used, :]
            for k, out in enumerate((down1, down2, down3)[:last], 1):
                out[...] = total[(last - k) * PLANE : (last - k + 1) * PLANE, :].astype(jnp.bfloat16)


def sum_values_kernel(own_ref, a_ref, b_ref, c_ref, out_ref):
    total = own_ref[...]
    for ref in (a_ref, b_ref, c_ref):
        total = total + ref[...].astype(jnp.float32)
    rounded = total.astype(jnp.bfloat16)
    for k in range(8):
        out_ref[k] = rounded


def gradient_kernel(behind, place, in_ref, v_ref, *refs):
    out_ref, own_ref, values, rows_a, rows_b = refs[behind:]
    zl = pl.program_id(0)

    @pl.when(zl == 0)
    def _():
        for c in range(2):
            for g in range(KV):
                values[c * PLANE : (c + 1) * PLANE, g * HD : (g + 1) * HD] = v_ref[c * KV + g]

    for half, rows in enumerate((rows_a, rows_b)):
        lhs = in_ref[:, half * 128 : half * 128 + 128]
        rows[...] = lax.dot_general(lhs, values[...], TN, preferred_element_type=jnp.float32)
    for to in range(16):
        part = jnp.concatenate([rows_a[8 * to : 8 * to + 8, :], rows_b[8 * to : 8 * to + 8, :]], axis=0)
        out_ref[to, 0] = part.astype(jnp.bfloat16)

    @pl.when(zl == place[ZL])
    def _():
        mine = pl.ds(pl.multiple_of((place[ZH] * 8 + place[Y]) * 8, 8), 8)
        own_ref[0:8, :] = rows_a[mine, :]
        own_ref[8:16, :] = rows_b[mine, :]


def gradient_terms(place, pieces, values, behind):
    columns = KV * HD
    parts, own = pl.pallas_call(
        functools.partial(gradient_kernel, len(behind)),
        grid=(4,),
        out_shape=(shape(16, 4, 16, columns), shape(16, columns, dtype=jnp.float32)),
        in_specs=[
            SCALARS,
            pl.BlockSpec((2 * PLANE, 256), lambda i: (0, i)),
            pl.BlockSpec((8, PLANE, HD), lambda i: (0, 0, 0)),
            *[ELSEWHERE] * len(behind),
        ],
        out_specs=(
            pl.BlockSpec((16, 1, 16, columns), lambda i: (0, i, 0, 0)),
            pl.BlockSpec((16, columns), lambda i: (0, 0)),
        ),
        scratch_shapes=[pltpu.VMEM((2 * PLANE, columns), jnp.bfloat16)] + [pltpu.VMEM((128, columns), jnp.float32)] * 2,
        compiler_params=pltpu.CompilerParams(vmem_limit_bytes=8 * MIB),
        cost_estimate=pl.CostEstimate(flops=1, bytes_accessed=1024, transcendentals=0),
        name="gradient",
    )(place, pieces, values, *behind)
    return parts.reshape(64, 16, columns), own


def sum_rows_kernel(place, in_ref, own_ref, out_ref):
    total = own_ref[...] - in_ref[place[ZH] * 32 + place[Y] * 4 + place[ZL]].astype(jnp.float32)
    for k in range(64):
        total = total + in_ref[k].astype(jnp.float32)
    for c in range(2):
        for half in range(2):
            part = total[half * 8 + c * 4 : half * 8 + c * 4 + 4, :]
            for k in range(16):
                out_ref[16 * c + k, half] = part


def order_kernel(place, old_owner, s0, s1, s2, s3, out_ref, count):
    for i in range(16):
        count[i] = 0

    @pl.loop(0, 64)
    def _(b):
        old = old_owner[b]
        slot = count[old]
        count[old] = slot + 1
        kx = (place[X] + 4 - old % 4) % 4
        for k, s_ref in enumerate((s0, s1, s2, s3)):

            @pl.when(kx == k)
            def _(s_ref=s_ref):
                rows = s_ref[old // 4, slot].astype(jnp.float32)
                out_ref[b, 0] = rows[0:4, :] + rows[4:8, :]
                out_ref[b, 1] = rows[8:12, :]
                out_ref[b, 2] = rows[12:16, :]


def update_kernel(place, new_owner, g_ref, st_ref, p_out, f_out, s_out, w_out, w_rows, changed, count):
    @pl.loop(0, 64, unroll=4)
    def _(b):
        owner = (b // 32) * 16 + ((b // 2) % 4) * 4 + (b // 8) % 4
        gradient = g_ref[owner, b % 2]
        param = st_ref[b, 0]
        first = beta_first * st_ref[b, 1] + (1.0 - beta_first) * gradient
        second = beta_second * st_ref[b, 2] + (1.0 - beta_second) * gradient * gradient
        first_hat = first / (1.0 - beta_first**STEP)
        second_hat = second / (1.0 - beta_second**STEP)
        param = param - learning_rate * (first_hat / (jnp.sqrt(second_hat) + epsilon) + decay_rate * param)
        for i in range(4):
            w_rows[i, pl.ds(b, 1), :] = param[i : i + 1, :]
        changed[b, 0] = param
        changed[b, 1] = first
        changed[b, 2] = second

    w_out[...] = w_rows[...].astype(jnp.bfloat16)
    count[0] = 0

    @pl.loop(0, 64)
    def _(b):
        @pl.when(new_owner[b] == place[ZL] * 4 + place[X])
        def _():
            to = count[0]
            count[0] = to + 1
            for part, out in enumerate((p_out, f_out, s_out)):
                block = changed[b, part]
                for i in range(4):
                    out[i, pl.ds(to, 1), :] = block[i : i + 1, :]


def local(queries, keys, grad_out, inputs, old_owner, new_owner, param_old, first_old, second_old):
    f32 = jnp.float32
    here = queries.shape[0]
    columns = KV * HD
    place = jnp.stack([lax.axis_index(a) for a in ("zh", "y", "c", "zl", "x")]).astype(jnp.int32)

    packed = call(pack_keys_kernel, "pack_keys", shape(KV, here, HD), [], [keys], [])
    plane_keys = swapped(packed, "x").reshape(PLANE, HD)
    packed = call(
        pack_heads_kernel, "pack_heads", shape(KV, here, 2 * GRP * HD), [], [queries, grad_out], []
    )
    heads = swapped(packed, "x")
    all_keys = [plane_keys, *(sent_up(plane_keys, k) for k in (1, 2, 3))]
    packed = call(
        pack_inputs_kernel, "pack_inputs", shape(8, here, 1024), [], [inputs], [], all_keys[1:]
    )
    pieces = swapped(packed, ("c", "x"))

    own, *parts = call(
        value_kernel,
        "values",
        (shape(PLANE, HD, dtype=f32), *(shape(PLANE, HD),) * 3),
        [place],
        [heads, *all_keys],
        [pltpu.VMEM((4 * PLANE, PLANE), f32)] * 2 + [pltpu.VMEM((4 * PLANE, HD), f32), pltpu.VMEM((1, PLANE), f32)],
        limit=16,
    )
    parts = [sent_down(parts[k - 1], k) for k in (1, 2, 3)]
    values = call(sum_values_kernel, "sum_values", shape(8, PLANE, HD), [], [own, *parts], [], [pieces])
    state = [a.transpose(1, 0, 2) for a in (param_old, first_old, second_old)]
    state = call(pack_states_kernel, "pack_states", shape(6, 16, columns), [], state, [], [values])
    planes = [state, *(old_planes(state, k) for k in (1, 2, 3))]
    values = swapped(values, ("c", "x"))

    parts, own = gradient_terms(place, pieces.reshape(2 * PLANE, 1024), values, planes[1:])
    state = call(join_planes_kernel, "join_planes", shape(3, 6, 16, columns), [place], planes, [])
    state = [state, *(shifted(state, "x", k) for k in (1, 2, 3))]
    arrived = swapped(parts, ("zh", "y", "zl"))
    rows = call(sum_rows_kernel, "sum_rows", shape(32, 2, 4, columns, dtype=f32), [place], [arrived, own], [], state[1:])
    state = call(
        order_kernel,
        "order",
        shape(64, 3, 4, columns, dtype=f32),
        [place, old_owner],
        state,
        [pltpu.SMEM((16,), jnp.int32)],
    )
    gradient = swapped(rows, ("c", "zl", "x"))
    block = shape(4, 4, columns, dtype=f32)
    return call(
        update_kernel,
        "update",
        (block, block, block, shape(4, 64, columns)),
        [place, new_owner],
        [gradient, state],
        [
            pltpu.VMEM((4, 64, columns), f32),
            pltpu.VMEM((64, 3, 4, columns), f32),
            pltpu.SMEM((1,), jnp.int32),
        ],
    )


def solution(mesh):
    fine = Mesh(mesh.devices.reshape(2, 8, 2, 4, 4), ("zh", "y", "c", "zl", "x"))
    rep = ("zh", "y", "c")
    shard = ("zl", "x")
    tokens = P((*rep, *shard), None)
    placed = (tokens,) * 4 + (P(), P()) + (P(rep, shard, None),) * 3
    return jax.shard_map(
        local,
        mesh=fine,
        in_specs=placed,
        out_specs=(P(rep, shard, None),) * 3 + (P(rep, None, None),),
        check_vma=False,
    )
```

```python
import functools

import jax
import jax.numpy as jnp
from jax import lax
from jax.experimental import pallas as pl
from jax.experimental.pallas import tpu as pltpu
from jax.sharding import Mesh, PartitionSpec as P

KV = 4
HD = 128
GRP = 8
STEP = 1000
LOG2E = 1.4426950408889634
MIB = 1 << 20

beta_first = 0.9
beta_second = 0.95
learning_rate = 0.02
decay_rate = 0.1
epsilon = 1e-08

PLANE = 512
CHUNK = 512
ZH, Y, C, ZL, X = range(5)
WHOLE = pl.BlockSpec(memory_space=pltpu.VMEM)
ELSEWHERE = pl.BlockSpec(memory_space=pl.ANY)
SCALARS = pl.BlockSpec(memory_space=pltpu.SMEM)
NT = (((1,), (1,)), ((), ()))
TN = (((0,), (0,)), ((), ()))


def swapped(x, axes):
    return lax.all_to_all(x, axes, split_axis=0, concat_axis=0, tiled=True)


def shifted(x, axis, k):
    n = lax.axis_size(axis)
    return lax.ppermute(x, axis, [(i, (i + k) % n) for i in range(n)])


def sent_up(x, k):
    return lax.ppermute(x, "zl", [(i, i + k) for i in range(4 - k)])


def sent_down(x, k):
    return lax.ppermute(x, "zl", [(i, i - k) for i in range(k, 4)])


def old_planes(x, k):
    return lax.ppermute(x, "zl", [(i, (i + k) % 4) for i in range(3)])


def call(kernel, name, out, scalars, arrays, scratch, behind=(), limit=8):
    given = len(scalars) + len(arrays)

    def body(*refs):
        kernel(*refs[:given], *refs[given + len(behind) :])

    return pl.pallas_call(
        body,
        out_shape=out,
        in_specs=[SCALARS] * len(scalars) + [WHOLE] * len(arrays) + [ELSEWHERE] * len(behind),
        out_specs=jax.tree.map(lambda _: WHOLE, out),
        scratch_shapes=scratch,
        compiler_params=pltpu.CompilerParams(vmem_limit_bytes=limit * MIB),
        cost_estimate=pl.CostEstimate(flops=1, bytes_accessed=1024, transcendentals=0),
        name=name,
    )(*scalars, *arrays, *behind)


def shape(*dims, dtype=jnp.bfloat16):
    return jax.ShapeDtypeStruct(dims, dtype)


def pack_heads_kernel(q_ref, d_ref, out_ref):
    width = GRP * HD
    for g in range(KV):
        out_ref[g, :, 0:width] = q_ref[:, g * width : (g + 1) * width]
        out_ref[g, :, width:] = d_ref[:, g * width : (g + 1) * width]


def pack_inputs_kernel(in_ref, out_ref):
    for k in range(8):
        out_ref[k] = in_ref[:, k * 1024 : (k + 1) * 1024]


def pack_keys_kernel(k_ref, out_ref):
    for g in range(KV):
        out_ref[g] = k_ref[:, g * HD : (g + 1) * HD]


def pack_states_kernel(p_ref, f_ref, s_ref, out_ref):
    for slot in range(6):
        param = p_ref[slot]
        high = param.astype(jnp.bfloat16).astype(jnp.float32)
        rows = jnp.concatenate([high, param - high, f_ref[slot], s_ref[slot]], axis=0)
        out_ref[slot] = rows.astype(jnp.bfloat16)


def join_planes_kernel(place, *refs):
    *from_planes, out_ref = refs
    for k, ref in enumerate(from_planes):
        plane = (place[ZL] + 4 - k) % 4

        @pl.when(plane < 3)
        def _(ref=ref, plane=plane):
            out_ref[plane] = ref[...]


def value_kernel(place, heads, k0, k1, k2, k3, own_ref, down1, down2, down3, s_a, s_b, total):
    plane = place[ZL]
    factor = HD**-0.5 * LOG2E
    width = GRP * HD

    def columns(start):
        at = pl.ds(pl.multiple_of(start, HD), HD)
        return heads[:, :, at].reshape(PLANE, HD)

    def scores(h, last, s_ref):
        q = columns(h * HD)
        top = jnp.full((8, PLANE), -jnp.inf, jnp.float32)
        for at in range(0, (last + 1) * PLANE, CHUNK):
            k_ref = (k0, k1, k2, k3)[last - at // PLANE]
            k = k_ref[at % PLANE : at % PLANE + CHUNK, :]
            s = lax.dot_general(k, q, NT, preferred_element_type=jnp.float32)
            if at >= last * PLANE:
                key = lax.broadcasted_iota(jnp.int32, s.shape, 0) + (at - last * PLANE)
                s = jnp.where(key <= lax.broadcasted_iota(jnp.int32, s.shape, 1), s, -jnp.inf)
            s_ref[at : at + CHUNK, :] = s
            top = jnp.maximum(top, jnp.max(s.reshape(CHUNK // 8, 8, PLANE), axis=0))
        return jnp.max(top, axis=0, keepdims=True)

    def add_terms(h, last, s_ref, top):
        d = columns(h * HD + width)
        size = jnp.zeros((8, PLANE), jnp.float32)
        for at in range(0, (last + 1) * PLANE, CHUNK):
            w = jnp.exp2((s_ref[at : at + CHUNK, :] - top) * factor)
            s_ref[at : at + CHUNK, :] = w
            size = size + jnp.sum(w.reshape(CHUNK // 8, 8, PLANE), axis=0)
        inverse = 1.0 / jnp.sum(size, axis=0, keepdims=True)
        for at in range(0, (last + 1) * PLANE, CHUNK):
            p = (s_ref[at : at + CHUNK, :] * inverse).astype(jnp.bfloat16)
            total[at : at + CHUNK, :] += jnp.dot(p, d, preferred_element_type=jnp.float32)

    for last in range(4):

        @pl.when(plane == last)
        def _(last=last):
            used = (last + 1) * PLANE
            total[0:used, :] = jnp.zeros((used, HD), jnp.float32)

            @pl.loop(0, GRP // 2)
            def _(pair):
                top_a = scores(2 * pair, last, s_a)
                top_b = scores(2 * pair + 1, last, s_b)
                add_terms(2 * pair, last, s_a, top_a)
                add_terms(2 * pair + 1, last, s_b, top_b)

            own_ref[...] = total[last * PLANE : used, :]
            for k, out in enumerate((down1, down2, down3)[:last], 1):
                out[...] = total[(last - k) * PLANE : (last - k + 1) * PLANE, :].astype(jnp.bfloat16)


def sum_values_kernel(own_ref, a_ref, b_ref, c_ref, out_ref):
    total = own_ref[...]
    for ref in (a_ref, b_ref, c_ref):
        total = total + ref[...].astype(jnp.float32)
    rounded = total.astype(jnp.bfloat16)
    for k in range(8):
        out_ref[k] = rounded


def gradient_kernel(behind, place, in_ref, v_ref, *refs):
    out_ref, own_ref, values, rows_a, rows_b = refs[behind:]
    zl = pl.program_id(0)

    @pl.when(zl == 0)
    def _():
        for c in range(2):
            for g in range(KV):
                values[c * PLANE : (c + 1) * PLANE, g * HD : (g + 1) * HD] = v_ref[c * KV + g]

    for half, rows in enumerate((rows_a, rows_b)):
        lhs = in_ref[:, half * 128 : half * 128 + 128]
        rows[...] = lax.dot_general(lhs, values[...], TN, preferred_element_type=jnp.float32)
    for to in range(16):
        part = jnp.concatenate([rows_a[8 * to : 8 * to + 8, :], rows_b[8 * to : 8 * to + 8, :]], axis=0)
        out_ref[to, 0] = part.astype(jnp.bfloat16)

    @pl.when(zl == place[ZL])
    def _():
        mine = pl.ds(pl.multiple_of((place[ZH] * 8 + place[Y]) * 8, 8), 8)
        own_ref[0:8, :] = rows_a[mine, :]
        own_ref[8:16, :] = rows_b[mine, :]


def gradient_terms(place, pieces, values, behind):
    columns = KV * HD
    parts, own = pl.pallas_call(
        functools.partial(gradient_kernel, len(behind)),
        grid=(4,),
        out_shape=(shape(16, 4, 16, columns), shape(16, columns, dtype=jnp.float32)),
        in_specs=[
            SCALARS,
            pl.BlockSpec((2 * PLANE, 256), lambda i: (0, i)),
            pl.BlockSpec((8, PLANE, HD), lambda i: (0, 0, 0)),
            *[ELSEWHERE] * len(behind),
        ],
        out_specs=(
            pl.BlockSpec((16, 1, 16, columns), lambda i: (0, i, 0, 0)),
            pl.BlockSpec((16, columns), lambda i: (0, 0)),
        ),
        scratch_shapes=[pltpu.VMEM((2 * PLANE, columns), jnp.bfloat16)] + [pltpu.VMEM((128, columns), jnp.float32)] * 2,
        compiler_params=pltpu.CompilerParams(vmem_limit_bytes=8 * MIB),
        cost_estimate=pl.CostEstimate(flops=1, bytes_accessed=1024, transcendentals=0),
        name="gradient",
    )(place, pieces, values, *behind)
    return parts.reshape(64, 16, columns), own


def sum_rows_kernel(place, in_ref, own_ref, out_ref):
    total = own_ref[...] - in_ref[place[ZH] * 32 + place[Y] * 4 + place[ZL]].astype(jnp.float32)
    for k in range(64):
        total = total + in_ref[k].astype(jnp.float32)
    for c in range(2):
        for half in range(2):
            part = total[half * 8 + c * 4 : half * 8 + c * 4 + 4, :]
            for k in range(16):
                out_ref[16 * c + k, half] = part


def order_kernel(place, old_owner, s0, s1, s2, s3, out_ref, count):
    for i in range(16):
        count[i] = 0

    @pl.loop(0, 64)
    def _(b):
        old = old_owner[b]
        slot = count[old]
        count[old] = slot + 1
        kx = (place[X] + 4 - old % 4) % 4
        for k, s_ref in enumerate((s0, s1, s2, s3)):

            @pl.when(kx == k)
            def _(s_ref=s_ref):
                rows = s_ref[old // 4, slot].astype(jnp.float32)
                out_ref[b, 0] = rows[0:4, :] + rows[4:8, :]
                out_ref[b, 1] = rows[8:12, :]
                out_ref[b, 2] = rows[12:16, :]


def update_kernel(place, new_owner, g_ref, st_ref, p_out, f_out, s_out, w_out, w_rows, changed, count):
    @pl.loop(0, 64, unroll=4)
    def _(b):
        owner = (b // 32) * 16 + ((b // 2) % 4) * 4 + (b // 8) % 4
        gradient = g_ref[owner, b % 2]
        param = st_ref[b, 0]
        first = beta_first * st_ref[b, 1] + (1.0 - beta_first) * gradient
        second = beta_second * st_ref[b, 2] + (1.0 - beta_second) * gradient * gradient
        first_hat = first / (1.0 - beta_first**STEP)
        second_hat = second / (1.0 - beta_second**STEP)
        param = param - learning_rate * (first_hat / (jnp.sqrt(second_hat) + epsilon) + decay_rate * param)
        for i in range(4):
            w_rows[i, pl.ds(b, 1), :] = param[i : i + 1, :]
        changed[b, 0] = param
        changed[b, 1] = first
        changed[b, 2] = second

    w_out[...] = w_rows[...].astype(jnp.bfloat16)
    count[0] = 0

    @pl.loop(0, 64)
    def _(b):
        @pl.when(new_owner[b] == place[ZL] * 4 + place[X])
        def _():
            to = count[0]
            count[0] = to + 1
            for part, out in enumerate((p_out, f_out, s_out)):
                block = changed[b, part]
                for i in range(4):
                    out[i, pl.ds(to, 1), :] = block[i : i + 1, :]


def local(queries, keys, grad_out, inputs, old_owner, new_owner, param_old, first_old, second_old):
    f32 = jnp.float32
    here = queries.shape[0]
    columns = KV * HD
    place = jnp.stack([lax.axis_index(a) for a in ("zh", "y", "c", "zl", "x")]).astype(jnp.int32)

    packed = call(pack_keys_kernel, "pack_keys", shape(KV, here, HD), [], [keys], [])
    plane_keys = swapped(packed, "x").reshape(PLANE, HD)
    packed = call(
        pack_heads_kernel, "pack_heads", shape(KV, here, 2 * GRP * HD), [], [queries, grad_out], []
    )
    heads = swapped(packed, "x")
    all_keys = [plane_keys, *(sent_up(plane_keys, k) for k in (1, 2, 3))]
    packed = call(
        pack_inputs_kernel, "pack_inputs", shape(8, here, 1024), [], [inputs], [], all_keys[1:]
    )
    pieces = swapped(packed, ("c", "x"))

    own, *parts = call(
        value_kernel,
        "values",
        (shape(PLANE, HD, dtype=f32), *(shape(PLANE, HD),) * 3),
        [place],
        [heads, *all_keys],
        [pltpu.VMEM((4 * PLANE, PLANE), f32)] * 2 + [pltpu.VMEM((4 * PLANE, HD), f32)],
        limit=24,
    )
    parts = [sent_down(parts[k - 1], k) for k in (1, 2, 3)]
    values = call(sum_values_kernel, "sum_values", shape(8, PLANE, HD), [], [own, *parts], [], [pieces])
    state = [a.transpose(1, 0, 2) for a in (param_old, first_old, second_old)]
    state = call(pack_states_kernel, "pack_states", shape(6, 16, columns), [], state, [], [values])
    planes = [state, *(old_planes(state, k) for k in (1, 2, 3))]
    values = swapped(values, ("c", "x"))

    parts, own = gradient_terms(place, pieces.reshape(2 * PLANE, 1024), values, planes[1:])
    state = call(join_planes_kernel, "join_planes", shape(3, 6, 16, columns), [place], planes, [])
    state = [state, *(shifted(state, "x", k) for k in (1, 2, 3))]
    arrived = swapped(parts, ("zh", "y", "zl"))
    state = call(
        order_kernel,
        "order",
        shape(64, 3, 4, columns, dtype=f32),
        [place, old_owner],
        state,
        [pltpu.SMEM((16,), jnp.int32)],
    )
    rows = call(sum_rows_kernel, "sum_rows", shape(32, 2, 4, columns, dtype=f32), [place], [arrived, own], [], [state])
    gradient = swapped(rows, ("c", "zl", "x"))
    block = shape(4, 4, columns, dtype=f32)
    return call(
        update_kernel,
        "update",
        (block, block, block, shape(4, 64, columns)),
        [place, new_owner],
        [gradient, state],
        [
            pltpu.VMEM((4, 64, columns), f32),
            pltpu.VMEM((64, 3, 4, columns), f32),
            pltpu.SMEM((1,), jnp.int32),
        ],
    )


def solution(mesh):
    fine = Mesh(mesh.devices.reshape(2, 8, 2, 4, 4), ("zh", "y", "c", "zl", "x"))
    rep = ("zh", "y", "c")
    shard = ("zl", "x")
    tokens = P((*rep, *shard), None)
    placed = (tokens,) * 4 + (P(), P()) + (P(rep, shard, None),) * 3
    return jax.shard_map(
        local,
        mesh=fine,
        in_specs=placed,
        out_specs=(P(rep, shard, None),) * 3 + (P(rep, None, None),),
        check_vma=False,
    )
```

```python
import functools

import jax
import jax.numpy as jnp
from jax import lax
from jax.experimental import pallas as pl
from jax.experimental.pallas import tpu as pltpu
from jax.sharding import Mesh, PartitionSpec as P

KV = 4
HD = 128
GRP = 8
STEP = 1000
LOG2E = 1.4426950408889634
MIB = 1 << 20

beta_first = 0.9
beta_second = 0.95
learning_rate = 0.02
decay_rate = 0.1
epsilon = 1e-08

PLANE = 512
CHUNK = 512
ZH, Y, C, ZL, X = range(5)
WHOLE = pl.BlockSpec(memory_space=pltpu.VMEM)
ELSEWHERE = pl.BlockSpec(memory_space=pl.ANY)
SCALARS = pl.BlockSpec(memory_space=pltpu.SMEM)
NT = (((1,), (1,)), ((), ()))
TN = (((0,), (0,)), ((), ()))


def swapped(x, axes):
    return lax.all_to_all(x, axes, split_axis=0, concat_axis=0, tiled=True)


def shifted(x, axis, k):
    n = lax.axis_size(axis)
    return lax.ppermute(x, axis, [(i, (i + k) % n) for i in range(n)])


def sent_up(x, k):
    return lax.ppermute(x, "zl", [(i, i + k) for i in range(4 - k)])


def sent_down(x, k):
    return lax.ppermute(x, "zl", [(i, i - k) for i in range(k, 4)])


def old_planes(x, k):
    return lax.ppermute(x, "zl", [(i, (i + k) % 4) for i in range(3)])


def call(kernel, name, out, scalars, arrays, scratch, behind=(), limit=8, elsewhere=()):
    given = len(scalars) + len(arrays) + len(elsewhere)

    def body(*refs):
        kernel(*refs[:given], *refs[given + len(behind) :])

    return pl.pallas_call(
        body,
        out_shape=out,
        in_specs=[SCALARS] * len(scalars) + [WHOLE] * len(arrays) + [ELSEWHERE] * len((*elsewhere, *behind)),
        out_specs=jax.tree.map(lambda _: WHOLE, out),
        scratch_shapes=scratch,
        compiler_params=pltpu.CompilerParams(vmem_limit_bytes=limit * MIB),
        cost_estimate=pl.CostEstimate(flops=1, bytes_accessed=1024, transcendentals=0),
        name=name,
    )(*scalars, *arrays, *elsewhere, *behind)


def shape(*dims, dtype=jnp.bfloat16):
    return jax.ShapeDtypeStruct(dims, dtype)


def pack_heads_kernel(q_ref, d_ref, out_ref):
    width = GRP * HD
    for g in range(KV):
        out_ref[g, :, 0:width] = q_ref[:, g * width : (g + 1) * width]
        out_ref[g, :, width:] = d_ref[:, g * width : (g + 1) * width]


def pack_inputs_kernel(in_ref, out_ref):
    for k in range(8):
        out_ref[k] = in_ref[:, k * 1024 : (k + 1) * 1024]


def pack_keys_kernel(k_ref, out_ref):
    for g in range(KV):
        out_ref[g] = k_ref[:, g * HD : (g + 1) * HD]


def pack_states_kernel(p_ref, f_ref, s_ref, out_ref):
    for slot in range(6):
        param = p_ref[slot]
        high = param.astype(jnp.bfloat16).astype(jnp.float32)
        rows = jnp.concatenate([high, param - high, f_ref[slot], s_ref[slot]], axis=0)
        out_ref[slot] = rows.astype(jnp.bfloat16)


def join_planes_kernel(place, *refs):
    *from_planes, out_ref = refs
    for k, ref in enumerate(from_planes):
        plane = (place[ZL] + 4 - k) % 4

        @pl.when(plane < 3)
        def _(ref=ref, plane=plane):
            out_ref[plane] = ref[...]


def value_kernel(place, k0, k1, k2, k3, given, own_ref, down1, down2, down3, s_a, s_b, total, heads, done):
    plane = place[ZL]
    factor = HD**-0.5 * LOG2E
    width = GRP * HD

    copy = pltpu.make_async_copy(given, heads, done.at[0])
    copy.start()
    copy.wait()

    def columns(start):
        at = pl.ds(pl.multiple_of(start, HD), HD)
        return heads[:, :, at].reshape(PLANE, HD)

    def scores(h, last, s_ref):
        q = columns(h * HD)
        top = jnp.full((8, PLANE), -jnp.inf, jnp.float32)
        for at in range(0, (last + 1) * PLANE, CHUNK):
            k_ref = (k0, k1, k2, k3)[last - at // PLANE]
            k = k_ref[at % PLANE : at % PLANE + CHUNK, :]
            s = lax.dot_general(k, q, NT, preferred_element_type=jnp.float32)
            if at >= last * PLANE:
                key = lax.broadcasted_iota(jnp.int32, s.shape, 0) + (at - last * PLANE)
                s = jnp.where(key <= lax.broadcasted_iota(jnp.int32, s.shape, 1), s, -jnp.inf)
            s_ref[at : at + CHUNK, :] = s
            top = jnp.maximum(top, jnp.max(s.reshape(CHUNK // 8, 8, PLANE), axis=0))
        return jnp.max(top, axis=0, keepdims=True)

    def add_terms(h, last, s_ref, top):
        d = columns(h * HD + width)
        size = jnp.zeros((8, PLANE), jnp.float32)
        for at in range(0, (last + 1) * PLANE, CHUNK):
            w = jnp.exp2((s_ref[at : at + CHUNK, :] - top) * factor)
            s_ref[at : at + CHUNK, :] = w
            size = size + jnp.sum(w.reshape(CHUNK // 8, 8, PLANE), axis=0)
        inverse = 1.0 / jnp.sum(size, axis=0, keepdims=True)
        for at in range(0, (last + 1) * PLANE, CHUNK):
            p = (s_ref[at : at + CHUNK, :] * inverse).astype(jnp.bfloat16)
            total[at : at + CHUNK, :] += jnp.dot(p, d, preferred_element_type=jnp.float32)

    for last in range(4):

        @pl.when(plane == last)
        def _(last=last):
            used = (last + 1) * PLANE
            total[0:used, :] = jnp.zeros((used, HD), jnp.float32)

            @pl.loop(0, GRP // 2)
            def _(pair):
                top_a = scores(2 * pair, last, s_a)
                top_b = scores(2 * pair + 1, last, s_b)
                add_terms(2 * pair, last, s_a, top_a)
                add_terms(2 * pair + 1, last, s_b, top_b)

            own_ref[...] = total[last * PLANE : used, :]
            for k, out in enumerate((down1, down2, down3)[:last], 1):
                out[...] = total[(last - k) * PLANE : (last - k + 1) * PLANE, :].astype(jnp.bfloat16)


def sum_values_kernel(own_ref, a_ref, b_ref, c_ref, out_ref):
    total = own_ref[...]
    for ref in (a_ref, b_ref, c_ref):
        total = total + ref[...].astype(jnp.float32)
    rounded = total.astype(jnp.bfloat16)
    for k in range(8):
        out_ref[k] = rounded


def gradient_kernel(behind, place, in_ref, v_ref, *refs):
    out_ref, own_ref, values, rows_a, rows_b = refs[behind:]
    zl = pl.program_id(0)

    @pl.when(zl == 0)
    def _():
        for c in range(2):
            for g in range(KV):
                values[c * PLANE : (c + 1) * PLANE, g * HD : (g + 1) * HD] = v_ref[c * KV + g]

    for half, rows in enumerate((rows_a, rows_b)):
        lhs = in_ref[:, half * 128 : half * 128 + 128]
        rows[...] = lax.dot_general(lhs, values[...], TN, preferred_element_type=jnp.float32)
    for to in range(16):
        part = jnp.concatenate([rows_a[8 * to : 8 * to + 8, :], rows_b[8 * to : 8 * to + 8, :]], axis=0)
        out_ref[to, 0] = part.astype(jnp.bfloat16)

    @pl.when(zl == place[ZL])
    def _():
        mine = pl.ds(pl.multiple_of((place[ZH] * 8 + place[Y]) * 8, 8), 8)
        own_ref[0:8, :] = rows_a[mine, :]
        own_ref[8:16, :] = rows_b[mine, :]


def gradient_terms(place, pieces, values, behind):
    columns = KV * HD
    parts, own = pl.pallas_call(
        functools.partial(gradient_kernel, len(behind)),
        grid=(4,),
        out_shape=(shape(16, 4, 16, columns), shape(16, columns, dtype=jnp.float32)),
        in_specs=[
            SCALARS,
            pl.BlockSpec((2 * PLANE, 256), lambda i: (0, i)),
            pl.BlockSpec((8, PLANE, HD), lambda i: (0, 0, 0)),
            *[ELSEWHERE] * len(behind),
        ],
        out_specs=(
            pl.BlockSpec((16, 1, 16, columns), lambda i: (0, i, 0, 0)),
            pl.BlockSpec((16, columns), lambda i: (0, 0)),
        ),
        scratch_shapes=[pltpu.VMEM((2 * PLANE, columns), jnp.bfloat16)] + [pltpu.VMEM((128, columns), jnp.float32)] * 2,
        compiler_params=pltpu.CompilerParams(vmem_limit_bytes=8 * MIB),
        cost_estimate=pl.CostEstimate(flops=1, bytes_accessed=1024, transcendentals=0),
        name="gradient",
    )(place, pieces, values, *behind)
    return parts.reshape(64, 16, columns), own


def sum_rows_kernel(place, in_ref, own_ref, out_ref):
    total = own_ref[...] - in_ref[place[ZH] * 32 + place[Y] * 4 + place[ZL]].astype(jnp.float32)
    for k in range(64):
        total = total + in_ref[k].astype(jnp.float32)
    for c in range(2):
        for half in range(2):
            part = total[half * 8 + c * 4 : half * 8 + c * 4 + 4, :]
            for k in range(16):
                out_ref[16 * c + k, half] = part


def order_kernel(place, old_owner, s0, s1, s2, s3, out_ref, count):
    for i in range(16):
        count[i] = 0

    @pl.loop(0, 64)
    def _(b):
        old = old_owner[b]
        slot = count[old]
        count[old] = slot + 1
        kx = (place[X] + 4 - old % 4) % 4
        for k, s_ref in enumerate((s0, s1, s2, s3)):

            @pl.when(kx == k)
            def _(s_ref=s_ref):
                rows = s_ref[old // 4, slot].astype(jnp.float32)
                out_ref[b, 0] = rows[0:4, :] + rows[4:8, :]
                out_ref[b, 1] = rows[8:12, :]
                out_ref[b, 2] = rows[12:16, :]


def update_kernel(place, new_owner, g_ref, st_ref, p_out, f_out, s_out, w_out, w_rows, changed, count):
    @pl.loop(0, 64, unroll=8)
    def _(b):
        owner = (b // 32) * 16 + ((b // 2) % 4) * 4 + (b // 8) % 4
        gradient = g_ref[owner, b % 2]
        param = st_ref[b, 0]
        first = beta_first * st_ref[b, 1] + (1.0 - beta_first) * gradient
        second = beta_second * st_ref[b, 2] + (1.0 - beta_second) * gradient * gradient
        first_hat = first / (1.0 - beta_first**STEP)
        second_hat = second / (1.0 - beta_second**STEP)
        param = param - learning_rate * (first_hat / (jnp.sqrt(second_hat) + epsilon) + decay_rate * param)
        for i in range(4):
            w_rows[i, pl.ds(b, 1), :] = param[i : i + 1, :]
        changed[b, 0] = param
        changed[b, 1] = first
        changed[b, 2] = second

    w_out[...] = w_rows[...].astype(jnp.bfloat16)
    count[0] = 0

    @pl.loop(0, 64)
    def _(b):
        @pl.when(new_owner[b] == place[ZL] * 4 + place[X])
        def _():
            to = count[0]
            count[0] = to + 1
            for part, out in enumerate((p_out, f_out, s_out)):
                block = changed[b, part]
                for i in range(4):
                    out[i, pl.ds(to, 1), :] = block[i : i + 1, :]


def local(queries, keys, grad_out, inputs, old_owner, new_owner, param_old, first_old, second_old):
    f32 = jnp.float32
    here = queries.shape[0]
    columns = KV * HD
    place = jnp.stack([lax.axis_index(a) for a in ("zh", "y", "c", "zl", "x")]).astype(jnp.int32)

    packed = call(pack_keys_kernel, "pack_keys", shape(KV, here, HD), [], [keys], [])
    plane_keys = swapped(packed, "x").reshape(PLANE, HD)
    packed = call(
        pack_heads_kernel, "pack_heads", shape(KV, here, 2 * GRP * HD), [], [queries, grad_out], []
    )
    heads = swapped(packed, "x")
    all_keys = [plane_keys, *(sent_up(plane_keys, k) for k in (1, 2, 3))]
    packed = call(
        pack_inputs_kernel, "pack_inputs", shape(8, here, 1024), [], [inputs], [], all_keys[1:]
    )
    pieces = swapped(packed, ("c", "x"))

    own, *parts = call(
        value_kernel,
        "values",
        (shape(PLANE, HD, dtype=f32), *(shape(PLANE, HD),) * 3),
        [place],
        all_keys,
        [
            *[pltpu.VMEM((4 * PLANE, PLANE), f32)] * 2,
            pltpu.VMEM((4 * PLANE, HD), f32),
            pltpu.VMEM((KV, here, 2 * GRP * HD), jnp.bfloat16),
            pltpu.SemaphoreType.DMA((1,)),
        ],
        elsewhere=[heads],
        limit=56,
    )
    parts = [sent_down(parts[k - 1], k) for k in (1, 2, 3)]
    values = call(sum_values_kernel, "sum_values", shape(8, PLANE, HD), [], [own, *parts], [], [pieces])
    state = [a.transpose(1, 0, 2) for a in (param_old, first_old, second_old)]
    state = call(pack_states_kernel, "pack_states", shape(6, 16, columns), [], state, [], [values])
    planes = [state, *(old_planes(state, k) for k in (1, 2, 3))]
    values = swapped(values, ("c", "x"))

    parts, own = gradient_terms(place, pieces.reshape(2 * PLANE, 1024), values, planes[1:])
    state = call(join_planes_kernel, "join_planes", shape(3, 6, 16, columns), [place], planes, [])
    state = [state, *(shifted(state, "x", k) for k in (1, 2, 3))]
    arrived = swapped(parts, ("zh", "y", "zl"))
    state = call(
        order_kernel,
        "order",
        shape(64, 3, 4, columns, dtype=f32),
        [place, old_owner],
        state,
        [pltpu.SMEM((16,), jnp.int32)],
    )
    rows = call(sum_rows_kernel, "sum_rows", shape(32, 2, 4, columns, dtype=f32), [place], [arrived, own], [], [state])
    gradient = swapped(rows, ("c", "zl", "x"))
    block = shape(4, 4, columns, dtype=f32)
    return call(
        update_kernel,
        "update",
        (block, block, block, shape(4, 64, columns)),
        [place, new_owner],
        [gradient, state],
        [
            pltpu.VMEM((4, 64, columns), f32),
            pltpu.VMEM((64, 3, 4, columns), f32),
            pltpu.SMEM((1,), jnp.int32),
        ],
    )


def solution(mesh):
    fine = Mesh(mesh.devices.reshape(2, 8, 2, 4, 4), ("zh", "y", "c", "zl", "x"))
    rep = ("zh", "y", "c")
    shard = ("zl", "x")
    tokens = P((*rep, *shard), None)
    placed = (tokens,) * 4 + (P(), P()) + (P(rep, shard, None),) * 3
    return jax.shard_map(
        local,
        mesh=fine,
        in_specs=placed,
        out_specs=(P(rep, shard, None),) * 3 + (P(rep, None, None),),
        check_vma=False,
    )
```
